512 devices in a mesh: node: 32 (over z, y_hi, core), dp: 4 (over x), tensor: 4 (over y_lo).
Axes of the slice: x: 4, y: 8 (y_hi: 2, y_lo: 4; y = y_hi * 4 + y_lo), z: 8, core: 2. Of those that a mesh axis runs over, the one named last changes fastest.
Arguments:
- hidden: bfloat16 [65536, 1024], P(('node', 'dp'), 'tensor'), may hold values from -6 to 6
- cotangent: bfloat16 [65536, 8192], P(('node', 'dp'), 'tensor'), may hold values from -0.032958984 to 0.032958984
- feedback: bfloat16 [32, 1024, 8192], P('node', 'dp', 'tensor'), may hold values from -1.5 to 1.5
- chosen: int32 [32, 4, 4, 64], P('node', 'dp', 'tensor'), may hold values from 0 to 127, all different within a row
- momentum: float32 [4, 4, 128, 64, 64], P('dp', 'tensor', 'node'), may hold values from -0.75 to 0.75
Outputs:
- feedback_new: bfloat16 [32, 1024, 8192], P('node', 'dp', 'tensor')
- momentum_new: float32 [4, 4, 128, 64, 64], P('dp', 'tensor', 'node')
- step: bfloat16 [1024, 8192], P('dp', 'tensor')
The draws below stay inside these ranges and needn't reach their ends.
Inputs may be any that keep to these rules, and one draw needn't show every extreme that they name: `chosen`: each device's list names 64 distinct blocks of its shard. Block b of a shard is owned by node b // (128 / 32).
All inputs are finite; a program needn't handle non-finite values.
Results may differ from the reference program's by a relative error of at most 0.014.
Values may be sent and summed in bfloat16 or wider, within the bound.
No kernel may reach another device: no remote copies, remote signals or barrier semaphores. Data moves between devices by JAX's collectives and lax.ppermute only.
A program may use at most 64 MiB of HBM per device.

```python
import jax
import jax.numpy as jnp
from jax import lax

D = 8192
BLK = 64
F_DEV = 256
TOK_DEV = 512
FFW = 1024
TOKENS = 65536
NB = 128
K = 64
N_NODE = 32
N_DP = 4
N_TENSOR = 4


def block_levels(rng, dims, cuts, least, high):
    def one(axis_at, blocks):
        draws = jax.random.uniform(jax.random.fold_in(jax.random.fold_in(rng, 6), axis_at), (blocks,), jnp.float32, least / len(cuts), high / len(cuts))
        return jnp.repeat(jnp.exp(draws), dims[axis_at] // blocks).reshape((-1,) + (1,) * (len(dims) - axis_at - 1))

    factor_of = one(*cuts[0])
    for cut in cuts[1:]:
        factor_of = factor_of * one(*cut)
    return factor_of


def choose_distinct(rng, rows, count, top, lift):
    sequence = jax.random.permutation(jax.random.fold_in(rng, 1), count)
    favour = sequence
    for power in range(3):
        favour = favour * favour // count
    favour = favour * lift // count
    tickets = jax.random.randint(jax.random.fold_in(rng, 2), (rows, count), 0, 4096) + favour
    holders = jax.random.permutation(jax.random.fold_in(rng, 3), rows)[jnp.arange(count) % rows]
    tickets = jnp.where(jnp.arange(rows)[:, None] == holders[None, :], 1 << 14, tickets)
    score = tickets * count + jnp.arange(count)
    return lax.top_k(score.astype(jnp.int32), top)[1].astype(jnp.int32)


def bell_draw(rng, shape, deviation, reach, split=(), kind=jnp.bfloat16):
    result = deviation * jax.random.normal(rng, shape, jnp.float32)
    if split:
        result = result * block_levels(rng, shape, split, -0.22, 0.18)
    return jnp.clip(result, -reach, reach).astype(kind)


def setup_inputs(seed: int = 0) -> dict:
    keys = jax.random.split(jax.random.key(seed), 6)
    hidden = bell_draw(keys[0], (TOKENS, FFW), 1.0, 6.0, ((0, 128), (1, 4)))
    cotangent = bell_draw(keys[1], (TOKENS, D), (0.25 * (TOK_DEV * N_DP) ** -0.5), 0.032958984, ((0, 128), (1, 4)))
    feedback = bell_draw(keys[2], (N_NODE, FFW, D), 0.25, 1.5, ((0, 32), (1, 4), (2, 4)))
    chosen = choose_distinct(keys[3], N_NODE * N_DP * N_TENSOR, NB, K, 8192).reshape((N_NODE, N_DP, N_TENSOR, K))
    momentum = bell_draw(keys[4], (N_DP, N_TENSOR, NB, BLK, BLK), 0.125, 0.75, ((0, 4), (1, 4), (2, 32)), jnp.float32)
    return {"hidden": hidden, "cotangent": cotangent, "feedback": feedback, "chosen": chosen, "momentum": momentum}


decay_rate = 0.9


def to_blocks(full):
    rows_blk = F_DEV // BLK
    cols_blk = D // N_TENSOR // BLK
    shaped = full.reshape(N_DP, rows_blk, BLK, N_TENSOR, cols_blk, BLK)
    return shaped.transpose(0, 3, 1, 4, 2, 5).reshape(N_DP, N_TENSOR, NB, BLK, BLK)


def from_blocks(blocks):
    rows_blk = F_DEV // BLK
    cols_blk = D // N_TENSOR // BLK
    shaped = blocks.reshape(N_DP, N_TENSOR, rows_blk, cols_blk, BLK, BLK)
    return shaped.transpose(0, 2, 4, 1, 3, 5).reshape(F_DEV * N_DP, D)


def reference(hidden, cotangent, feedback, chosen, momentum):
    hidden_nodes = hidden.reshape(N_NODE, N_DP, TOK_DEV, F_DEV * N_DP)
    cot_nodes = cotangent.reshape(N_NODE, N_DP, TOK_DEV, D)

    def one_node(total, items):
        h_node, g_node, fb_node, pick_node = items
        partial_value = jnp.einsum("dtf,dte->dfe", h_node.astype(jnp.float32), g_node.astype(jnp.float32),
                             precision=lax.Precision.HIGHEST)
        partial_value = partial_value.astype(jnp.bfloat16).astype(jnp.float32)
        grad = jnp.sum(partial_value, axis=0)
        acc = fb_node.astype(jnp.float32) + grad
        acc_blocks = to_blocks(acc)
        mask = jnp.any(pick_node[..., None] == jnp.arange(NB, dtype=jnp.int32), axis=-2)
        sent = jnp.where(mask[..., None, None], acc_blocks, jnp.float32(0.0))
        kept = jnp.where(mask[..., None, None], jnp.float32(0.0), acc_blocks)
        return total + sent, from_blocks(kept).astype(jnp.bfloat16)

    start = jnp.zeros((N_DP, N_TENSOR, NB, BLK, BLK), jnp.float32)
    total, feedback_new = lax.scan(one_node, start, (hidden_nodes, cot_nodes, feedback, chosen))
    mean = total / N_NODE
    momentum_new = decay_rate * momentum + mean
    step = from_blocks(mean + decay_rate * momentum_new).astype(jnp.bfloat16)
    return feedback_new, momentum_new, step
```

```python
import jax
import jax.numpy as jnp
from jax import lax
from jax.sharding import Mesh, PartitionSpec as P

BLK = 64
DECAY = 0.9
F32, BF16 = jnp.float32, jnp.bfloat16
NODE = ("z", "yh", "c")
SHAPE = (8, 2, 2, 4, 4)


def swap(value, axis, flip, size):
    return lax.ppermute(value, axis, [(i, i ^ flip) for i in range(size)])


def sum_over_dp(hidden, cotangent):
    d, t = lax.axis_index("dp"), lax.axis_index("t")
    whole = [hidden]
    for shift in (1, 2, 3):
        whole.append(lax.ppermute(hidden, "t", [(i, (i + shift) % 4) for i in range(4)]))
    whole = jnp.stack(whole)
    half = cotangent.shape[1] // 2

    def part(flip, cols):
        rows = lax.dynamic_index_in_dim(whole, (t - (d ^ flip)) % 4, 0, keepdims=False)
        return lax.dot_general(
            rows, cols, (((0,), (0,)), ((), ())), preferred_element_type=F32
        ).astype(BF16)

    a, b = cotangent[:, :half], cotangent[:, half:]
    own_a, own_b = part(0, a), part(0, b)
    a1, a2, a3 = part(1, a), part(2, a), part(3, a)
    b1, b2, b3 = part(1, b), part(2, b), part(3, b)
    got_a = swap(jnp.stack([a1, a2]), "dp", 1, 4)
    got_b = swap(jnp.stack([b3, b2]), "dp", 3, 4)
    next_a = swap((a3.astype(F32) + got_a[1].astype(F32)).astype(BF16), "dp", 3, 4)
    next_b = swap((b1.astype(F32) + got_b[1].astype(F32)).astype(BF16), "dp", 1, 4)
    sum_a = own_a.astype(F32) + got_a[0].astype(F32) + next_a.astype(F32)
    sum_b = own_b.astype(F32) + got_b[0].astype(F32) + next_b.astype(F32)
    return jnp.concatenate([sum_a, sum_b], axis=1)


def local(hidden, cotangent, feedback, chosen, momentum):
    rows, cols = feedback.shape[1:]
    rows_blk, cols_blk = rows // BLK, cols // BLK
    nodes = 32
    c, yh = lax.axis_index("c"), lax.axis_index("yh")
    grad = sum_over_dp(hidden, cotangent)
    acc = feedback[0].astype(F32) + grad
    picks = chosen.reshape(-1)
    mask = jnp.any(
        picks[:, None] == jnp.arange(rows_blk * cols_blk, dtype=jnp.int32)[None, :], axis=0
    ).reshape(rows_blk, cols_blk)
    wide = jnp.repeat(mask, BLK, axis=1)
    wide = jnp.broadcast_to(wide[:, None, :], (rows_blk, BLK, cols)).reshape(rows, cols)
    feedback_new = jnp.where(wide, 0.0, acc).astype(BF16)[None]
    sent = jnp.where(wide, acc, 0.0)
    sent = sent.reshape(rows, 4, 2, 256)
    mine = lax.dynamic_index_in_dim(sent, c, 2, keepdims=False)
    other = lax.dynamic_index_in_dim(sent, 1 - c, 2, keepdims=False).astype(BF16)
    pair = (mine + swap(other, "c", 1, 2).astype(F32)).astype(BF16)
    pair = pair.reshape(4, BLK, 2, 2, 256).transpose(0, 2, 1, 3, 4).reshape(8, BLK, 512)
    got = lax.all_to_all(pair, "z", 0, 0, tiled=True)
    summed = jnp.sum(got.astype(F32), axis=0).reshape(BLK, 2, 256)
    keep = lax.dynamic_index_in_dim(summed, yh, 1, keepdims=False)
    give = lax.dynamic_index_in_dim(summed, 1 - yh, 1, keepdims=False)
    total = keep + swap(give, "yh", 1, 2)
    mean = total.reshape(BLK, 4, BLK).transpose(1, 0, 2) / nodes
    momentum_new = DECAY * momentum[0, 0] + mean
    step = (mean + DECAY * momentum_new).astype(BF16)
    step = step.transpose(1, 0, 2).reshape(BLK, 256)
    peer = swap(step, "yh", 1, 2)
    both = jnp.where(yh == 0, jnp.concatenate([step, peer], 1), jnp.concatenate([peer, step], 1))
    every = lax.all_gather(both, "z", axis=0)
    far = swap(every, "c", 1, 2)
    first, second = jnp.where(c == 0, every, far), jnp.where(c == 0, far, every)
    out = jnp.stack([first.reshape(4, 2, BLK, 2, 256), second.reshape(4, 2, BLK, 2, 256)], axis=4)
    out = out.transpose(0, 2, 1, 3, 4, 5).reshape(rows, cols)
    return feedback_new, momentum_new[None, None], out


def solution(mesh):
    fine = Mesh(mesh.devices.reshape(SHAPE), (*NODE, "dp", "t"))
    tokens = P((*NODE, "dp"), "t")
    return jax.shard_map(
        local,
        mesh=fine,
        in_specs=(
            tokens,
            tokens,
            P(NODE, "dp", "t"),
            P(NODE, "dp", "t", None),
            P("dp", "t", NODE, None, None),
        ),
        out_specs=(P(NODE, "dp", "t"), P("dp", "t", NODE, None, None), P("dp", "t")),
        check_vma=False,
    )
```

```python
import jax
import jax.numpy as jnp
from jax import lax
from jax.experimental import pallas as pl
from jax.experimental.pallas import tpu as pltpu
from jax.sharding import Mesh, PartitionSpec as P

BLK = 64
DECAY = 0.9
NODES = 32
F32, BF16 = jnp.float32, jnp.bfloat16
NODE = ("z", "yh", "c")
SHAPE = (8, 2, 2, 4, 4)
VMEM_LIMIT = 32 * 1024 * 1024


def swap(value, axis, flip, size):
    return lax.ppermute(value, axis, [(i, i ^ flip) for i in range(size)])


def kernel_call(body, grid, ins, outs, out_shape, cost):
    return pl.pallas_call(
        body,
        grid=grid,
        in_specs=ins,
        out_specs=outs,
        out_shape=out_shape,
        compiler_params=pltpu.CompilerParams(vmem_limit_bytes=VMEM_LIMIT),
        cost_estimate=pl.CostEstimate(flops=cost, bytes_accessed=cost, transcendentals=0),
    )


SMEM = pl.BlockSpec(memory_space=pltpu.SMEM)


def feedback_kernel(
    c_ref, mask_ref, fb_ref, own_ref, got_a, got_b, next_a, next_b, new_ref, mine_ref, other_ref
):
    first = c_ref[0] == 0
    for h, got, nxt in ((0, got_a, next_a), (1, got_b, next_b)):
        for yh in range(2):
            sent = []
            for c in range(2):
                near = slice(yh * 512 + c * 256, yh * 512 + c * 256 + 256)
                far = slice(h * 1024 + near.start, h * 1024 + near.stop)
                acc = (
                    own_ref[:, far].astype(F32)
                    + got[0, :, near].astype(F32)
                    + nxt[:, near].astype(F32)
                )
                acc = fb_ref[:, far].astype(F32) + acc
                chosen = jnp.broadcast_to(mask_ref[0, :, far], acc.shape) > 0.5
                new_ref[:, far] = jnp.where(chosen, 0.0, acc).astype(BF16)
                sent.append(jnp.where(chosen, acc, 0.0))
            place = slice(yh * 256, yh * 256 + 256)
            mine_ref[h, :, place] = jnp.where(first, sent[0], sent[1])
            other_ref[h, :, place] = jnp.where(first, sent[1], sent[0]).astype(BF16)


def error_feedback(c, mask, feedback, own, got_a, got_b, next_a, next_b):
    rows, cols = feedback.shape
    groups = rows // BLK
    wide = pl.BlockSpec((BLK, cols), lambda i: (i, 0))
    half = pl.BlockSpec((BLK, cols // 2), lambda i: (i, 0))
    slab = pl.BlockSpec((2, BLK, 512), lambda i: (i, 0, 0))
    line = pl.BlockSpec((1, 1, cols), lambda i: (i, 0, 0))
    got = pl.BlockSpec((1, BLK, cols // 2), lambda i: (0, i, 0))
    return kernel_call(
        feedback_kernel,
        (groups,),
        [SMEM, line, wide, wide, got, got, half, half],
        [wide, slab, slab],
        [
            jax.ShapeDtypeStruct((rows, cols), BF16),
            jax.ShapeDtypeStruct((2 * groups, BLK, 512), F32),
            jax.ShapeDtypeStruct((2 * groups, BLK, 512), BF16),
        ],
        8 * rows * cols,
    )(c, mask, feedback, own, got_a, got_b, next_a, next_b)


def owner_kernel(yh_ref, mine_ref, peer_ref, moment_ref, new_ref, step_ref):
    mean = (mine_ref[...] + peer_ref[...]) * (1.0 / NODES)
    moment = DECAY * moment_ref[...] + mean
    step = (mean + DECAY * moment).astype(BF16)
    for z in range(8):
        step_ref[z] = step
    own = jnp.where(yh_ref[0] == 0, moment[:, :256], moment[:, 256:])
    for b in range(4):
        new_ref[b] = own[:, b * BLK : (b + 1) * BLK]


def owner_update(yh, mine, peer, moment):
    whole = pl.BlockSpec(memory_space=pltpu.VMEM)
    return kernel_call(
        owner_kernel,
        (),
        [SMEM, whole, whole, whole],
        [whole, whole],
        [
            jax.ShapeDtypeStruct((4, BLK, BLK), F32),
            jax.ShapeDtypeStruct((8, BLK, 512), BF16),
        ],
        8 * BLK * 512,
    )(yh, mine, peer, moment)


def assemble_kernel(c_ref, mine_ref, other_ref, out_ref):
    first = c_ref[0] == 0
    for h in range(2):
        for yh in range(2):
            place = slice(yh * 256, yh * 256 + 256)
            mine, other = mine_ref[h, :, place], other_ref[h, :, place]
            at = h * 1024 + yh * 512
            out_ref[:, at : at + 256] = jnp.where(first, mine, other)
            out_ref[:, at + 256 : at + 512] = jnp.where(first, other, mine)


def assemble(c, mine, other, rows, cols):
    slab = pl.BlockSpec((2, BLK, 512), lambda i: (i, 0, 0))
    return kernel_call(
        assemble_kernel,
        (rows // BLK,),
        [SMEM, slab, slab],
        pl.BlockSpec((BLK, cols), lambda i: (i, 0)),
        jax.ShapeDtypeStruct((rows, cols), BF16),
        4 * rows * cols,
    )(c, mine, other)


def partial_sums(hidden, cotangent, early):
    d, t = lax.axis_index("dp"), lax.axis_index("t")
    whole = [hidden]
    for shift in (1, 2, 3):
        whole.append(lax.ppermute(hidden, "t", [(i, (i + shift) % 4) for i in range(4)]))
    *whole, early = lax.optimization_barrier((*whole, early))
    whole = jnp.stack(whole)

    def part(flip, cols):
        rows = lax.dynamic_index_in_dim(whole, (t - (d ^ flip)) % 4, 0, keepdims=False)
        return lax.dot_general(
            rows, cols, (((0,), (0,)), ((), ())), preferred_element_type=F32
        ).astype(BF16)

    half = cotangent.shape[1] // 2
    a, b = cotangent[:, :half], cotangent[:, half:]
    a1, a2, a3 = part(1, a), part(2, a), part(3, a)
    b1, b2, b3 = part(1, b), part(2, b), part(3, b)
    own = part(0, cotangent)
    got_a = swap(jnp.stack([a1, a2]), "dp", 1, 4)
    got_b = swap(jnp.stack([b3, b2]), "dp", 3, 4)
    next_a = swap((a3.astype(F32) + got_a[1].astype(F32)).astype(BF16), "dp", 3, 4)
    next_b = swap((b1.astype(F32) + got_b[1].astype(F32)).astype(BF16), "dp", 1, 4)
    return early, own, got_a, got_b, next_a, next_b


def as_matrix(blocks):
    return blocks.transpose(1, 0, 2).reshape(BLK, -1)


def local(hidden, cotangent, feedback, chosen, momentum):
    rows, cols = feedback.shape[1:]
    rows_blk, cols_blk = rows // BLK, cols // BLK
    c, yh = lax.axis_index("c"), lax.axis_index("yh")
    at_c, at_yh = c.astype(jnp.int32).reshape(1), yh.astype(jnp.int32).reshape(1)
    block_of = (
        jnp.arange(rows_blk, dtype=jnp.int32)[:, None] * cols_blk
        + jnp.arange(cols, dtype=jnp.int32)[None, :] // BLK
    )
    mask = jnp.any(chosen.reshape(-1, 1, 1) == block_of[None], axis=0).astype(F32)
    moment = as_matrix(momentum[0, 0])
    far_moment = swap(moment, "yh", 1, 2)
    far_moment, *parts = partial_sums(hidden, cotangent, far_moment)
    moment = jnp.where(
        yh == 0, jnp.concatenate([moment, far_moment], 1), jnp.concatenate([far_moment, moment], 1)
    )
    feedback_new, mine, other = error_feedback(at_c, mask[:, None], feedback[0], *parts)
    pair = (mine + swap(other, "c", 1, 2).astype(F32)).astype(BF16)
    got = lax.all_to_all(pair, "z", 0, 0, tiled=True)
    near = jnp.sum(got.astype(F32), axis=0)
    momentum_new, copies = owner_update(at_yh, near, swap(near, "yh", 1, 2), moment)
    every = lax.all_to_all(copies, "z", 0, 0, tiled=True)
    step = assemble(at_c, every, swap(every, "c", 1, 2), rows, cols)
    return feedback_new[None], momentum_new[None, None], step


def solution(mesh):
    fine = Mesh(mesh.devices.reshape(SHAPE), (*NODE, "dp", "t"))
    tokens = P((*NODE, "dp"), "t")
    return jax.shard_map(
        local,
        mesh=fine,
        in_specs=(
            tokens,
            tokens,
            P(NODE, "dp", "t"),
            P(NODE, "dp", "t", None),
            P("dp", "t", NODE, None, None),
        ),
        out_specs=(P(NODE, "dp", "t"), P("dp", "t", NODE, None, None), P("dp", "t")),
        check_vma=False,
    )
```

```python
import jax
import jax.numpy as jnp
from jax import lax
from jax.experimental import pallas as pl
from jax.experimental.pallas import tpu as pltpu
from jax.sharding import Mesh, PartitionSpec as P

BLK = 64
DECAY = 0.9
CHUNKS = 2
NODES = 32
F32, BF16 = jnp.float32, jnp.bfloat16
NODE = ("z", "yh", "c")
SHAPE = (8, 2, 2, 4, 4)
VMEM_LIMIT = 32 * 1024 * 1024


def swap(value, axis, flip, size):
    return lax.ppermute(value, axis, [(i, i ^ flip) for i in range(size)])


def kernel_call(body, grid, ins, outs, out_shape, cost):
    return pl.pallas_call(
        body,
        grid=grid,
        in_specs=ins,
        out_specs=outs,
        out_shape=out_shape,
        compiler_params=pltpu.CompilerParams(vmem_limit_bytes=VMEM_LIMIT),
        cost_estimate=pl.CostEstimate(flops=cost, bytes_accessed=cost, transcendentals=0),
    )


SMEM = pl.BlockSpec(memory_space=pltpu.SMEM)


def feedback_kernel(
    c_ref, mask_ref, fb_ref, own_ref, got_a, got_b, next_a, next_b, _, new_ref, mine_ref, other_ref
):
    first = c_ref[0] == 0
    for h, got, nxt in ((0, got_a, next_a), (1, got_b, next_b)):
        for yh in range(2):
            sent = []
            for c in range(2):
                near = slice(yh * 512 + c * 256, yh * 512 + c * 256 + 256)
                far = slice(h * 1024 + near.start, h * 1024 + near.stop)
                acc = (
                    own_ref[:, far].astype(F32)
                    + got[0, :, near].astype(F32)
                    + nxt[:, near].astype(F32)
                )
                acc = fb_ref[:, far].astype(F32) + acc
                chosen = jnp.broadcast_to(mask_ref[0, :, far], acc.shape) > 0.5
                new_ref[:, far] = jnp.where(chosen, 0.0, acc).astype(BF16)
                sent.append(jnp.where(chosen, acc, 0.0))
            place = slice(yh * 256, yh * 256 + 256)
            mine_ref[h, :, place] = jnp.where(first, sent[0], sent[1])
            other_ref[h, :, place] = jnp.where(first, sent[1], sent[0]).astype(BF16)


def error_feedback(chunk, c, mask, feedback, own, got_a, got_b, next_a, next_b, new):
    cols = feedback.shape[1]
    groups = own.shape[0] // BLK
    base = chunk * groups
    line = pl.BlockSpec((1, 1, cols), lambda i: (base + i, 0, 0))
    state = pl.BlockSpec((BLK, cols), lambda i: (base + i, 0))
    wide = pl.BlockSpec((BLK, cols), lambda i: (i, 0))
    half = pl.BlockSpec((BLK, cols // 2), lambda i: (i, 0))
    slab = pl.BlockSpec((2, BLK, 512), lambda i: (i, 0, 0))
    got = pl.BlockSpec((1, BLK, cols // 2), lambda i: (0, i, 0))
    return pl.pallas_call(
        feedback_kernel,
        grid=(groups,),
        in_specs=[SMEM, line, state, wide, got, got, half, half, pl.BlockSpec(memory_space=pl.ANY)],
        out_specs=[state, slab, slab],
        out_shape=[
            jax.ShapeDtypeStruct(feedback.shape, BF16),
            jax.ShapeDtypeStruct((2 * groups, BLK, 512), F32),
            jax.ShapeDtypeStruct((2 * groups, BLK, 512), BF16),
        ],
        input_output_aliases={8: 0},
        compiler_params=pltpu.CompilerParams(vmem_limit_bytes=VMEM_LIMIT),
        cost_estimate=pl.CostEstimate(flops=1 << 22, bytes_accessed=1 << 22, transcendentals=0),
    )(c, mask, feedback, own, got_a, got_b, next_a, next_b, new)


def owner_kernel(yh_ref, mine_ref, peer_ref, moment_ref, new_ref, step_ref):
    mean = (mine_ref[...].astype(F32) + peer_ref[...].astype(F32)) * (1.0 / NODES)
    moment = DECAY * moment_ref[...] + mean
    step = (mean + DECAY * moment).astype(BF16)
    for z in range(8):
        step_ref[z] = step
    own = jnp.where(yh_ref[0] == 0, moment[:, :256], moment[:, 256:])
    for b in range(4):
        new_ref[b] = own[:, b * BLK : (b + 1) * BLK]


def owner_update(yh, mine, peer, moment):
    whole = pl.BlockSpec(memory_space=pltpu.VMEM)
    return kernel_call(
        owner_kernel,
        (),
        [SMEM, whole, whole, whole],
        [whole, whole],
        [
            jax.ShapeDtypeStruct((4, BLK, BLK), F32),
            jax.ShapeDtypeStruct((8, BLK, 512), BF16),
        ],
        8 * BLK * 512,
    )(yh, mine, peer, moment)


def assemble_kernel(c_ref, mine_ref, other_ref, out_ref):
    first = c_ref[0] == 0
    for h in range(2):
        for yh in range(2):
            place = slice(yh * 256, yh * 256 + 256)
            mine, other = mine_ref[h, :, place], other_ref[h, :, place]
            at = h * 1024 + yh * 512
            out_ref[:, at : at + 256] = jnp.where(first, mine, other)
            out_ref[:, at + 256 : at + 512] = jnp.where(first, other, mine)


def assemble(c, mine, other, rows, cols):
    slab = pl.BlockSpec((2, BLK, 512), lambda i: (i, 0, 0))
    return kernel_call(
        assemble_kernel,
        (rows // BLK,),
        [SMEM, slab, slab],
        pl.BlockSpec((BLK, cols), lambda i: (i, 0)),
        jax.ShapeDtypeStruct((rows, cols), BF16),
        4 * rows * cols,
    )(c, mine, other)


def ring_shift(value, shift):
    return lax.ppermute(value, "t", [(i, (i + shift) % 4) for i in range(4)])


def products(shards, cotangent):
    d, t = lax.axis_index("dp"), lax.axis_index("t")
    shards = jnp.stack(shards)
    half = cotangent.shape[1] // 2

    def part(flip, cols):
        rows = lax.dynamic_index_in_dim(shards, (t - (d ^ flip)) % 4, 0, keepdims=False)
        return lax.dot_general(
            rows, cols, (((0,), (0,)), ((), ())), preferred_element_type=F32
        ).astype(BF16)

    a, b = cotangent[:, :half], cotangent[:, half:]
    send_a = jnp.stack([part(1, a), part(2, a)])
    send_b = jnp.stack([part(3, b), part(2, b)])
    return send_a, send_b, part(3, a), part(1, b), part(0, cotangent)


def plus(kept, got):
    return (kept.astype(F32) + got[1].astype(F32)).astype(BF16)


def as_matrix(blocks):
    return blocks.transpose(1, 0, 2).reshape(BLK, -1)


def local(hidden, cotangent, feedback, chosen, momentum):
    rows, cols = feedback.shape[1:]
    rows_blk, cols_blk = rows // BLK, cols // BLK
    c, yh = lax.axis_index("c"), lax.axis_index("yh")
    at_c, at_yh = c.astype(jnp.int32).reshape(1), yh.astype(jnp.int32).reshape(1)
    block_of = (
        jnp.arange(rows_blk, dtype=jnp.int32)[:, None] * cols_blk
        + jnp.arange(cols, dtype=jnp.int32)[None, :] // BLK
    )
    mask = jnp.any(chosen.reshape(-1, 1, 1) == block_of[None], axis=0).astype(F32)
    width = hidden.shape[1] // CHUNKS
    shards = []
    for r in range(CHUNKS):
        piece = hidden[:, r * width : (r + 1) * width]
        shards.append([piece] + [ring_shift(piece, k) for k in (1, 2, 3)])
    moment = as_matrix(momentum[0, 0])
    far_moment = swap(moment, "yh", 1, 2)
    work = [products(shards[0], cotangent)]
    *held, far_moment = lax.optimization_barrier((*shards[1], far_moment, work[0][0], work[0][1]))[:5]
    work.append(products(held, cotangent))
    moment = jnp.where(
        yh == 0, jnp.concatenate([moment, far_moment], 1), jnp.concatenate([far_moment, moment], 1)
    )
    got = [(swap(w[0], "dp", 1, 4), swap(w[1], "dp", 3, 4)) for w in work]
    feedback_new = jnp.zeros((rows, cols), BF16)
    own = [w[4] for w in work]
    got_a, mask, feedback_new, *own = lax.optimization_barrier((got[0][0], mask, feedback_new, *own))
    got[0] = (got_a, got[0][1])
    after = [
        (swap(plus(w[2], g[0]), "dp", 3, 4), swap(plus(w[3], g[1]), "dp", 1, 4))
        for w, g in zip(work, got)
    ]
    pairs = []
    for r in range(CHUNKS):
        feedback_new, mine, other = error_feedback(
            r, at_c, mask[:, None], feedback[0], own[r], *got[r], *after[r], feedback_new
        )
        pairs.append((mine + swap(other, "c", 1, 2).astype(F32)).astype(BF16))
    across = lax.all_to_all(jnp.concatenate(pairs), "z", 0, 0, tiled=True)
    near = jnp.sum(across.astype(F32), axis=0).astype(BF16)
    momentum_new, copies = owner_update(at_yh, near, swap(near, "yh", 1, 2), moment)
    every = lax.all_to_all(copies, "z", 0, 0, tiled=True)
    step = assemble(at_c, every, swap(every, "c", 1, 2), rows, cols)
    return feedback_new[None], momentum_new[None, None], step


def solution(mesh):
    fine = Mesh(mesh.devices.reshape(SHAPE), (*NODE, "dp", "t"))
    tokens = P((*NODE, "dp"), "t")
    return jax.shard_map(
        local,
        mesh=fine,
        in_specs=(
            tokens,
            tokens,
            P(NODE, "dp", "t"),
            P(NODE, "dp", "t", None),
            P("dp", "t", NODE, None, None),
        ),
        out_specs=(P(NODE, "dp", "t"), P("dp", "t", NODE, None, None), P("dp", "t")),
        check_vma=False,
    )
```

```python
import jax
import jax.numpy as jnp
from jax import lax
from jax.experimental import pallas as pl
from jax.experimental.pallas import tpu as pltpu
from jax.sharding import Mesh, PartitionSpec as P

BLK = 64
DECAY = 0.9
NODES = 32
F32, BF16 = jnp.float32, jnp.bfloat16
NODE = ("z", "yh", "c")
SHAPE = (8, 2, 2, 4, 4)
VMEM_LIMIT = 32 * 1024 * 1024


def swap(value, axis, flip, size):
    return lax.ppermute(value, axis, [(i, i ^ flip) for i in range(size)])


def kernel_call(body, grid, ins, outs, out_shape, cost):
    return pl.pallas_call(
        body,
        grid=grid,
        in_specs=ins,
        out_specs=outs,
        out_shape=out_shape,
        compiler_params=pltpu.CompilerParams(vmem_limit_bytes=VMEM_LIMIT),
        cost_estimate=pl.CostEstimate(flops=cost, bytes_accessed=cost, transcendentals=0),
    )


SMEM = pl.BlockSpec(memory_space=pltpu.SMEM)


def feedback_kernel(
    c_ref, mask_ref, fb_ref, own_ref, got_a, got_b, next_a, next_b, new_ref, mine_ref, other_ref
):
    first = c_ref[0] == 0
    for h, got, nxt in ((0, got_a, next_a), (1, got_b, next_b)):
        for yh in range(2):
            sent = []
            for c in range(2):
                near = slice(yh * 512 + c * 256, yh * 512 + c * 256 + 256)
                far = slice(h * 1024 + near.start, h * 1024 + near.stop)
                acc = (
                    own_ref[:, far].astype(F32)
                    + got[:, near].astype(F32)
                    + nxt[:, near].astype(F32)
                )
                acc = fb_ref[:, far].astype(F32) + acc
                chosen = jnp.broadcast_to(mask_ref[0, :, far], acc.shape) > 0.5
                new_ref[:, far] = jnp.where(chosen, 0.0, acc).astype(BF16)
                sent.append(jnp.where(chosen, acc, 0.0))
            place = slice(yh * 256, yh * 256 + 256)
            mine_ref[h, :, place] = jnp.where(first, sent[0], sent[1])
            other_ref[h, :, place] = jnp.where(first, sent[1], sent[0]).astype(BF16)


def error_feedback(c, mask, feedback, own, got_a, got_b, next_a, next_b):
    rows, cols = feedback.shape
    groups = rows // BLK
    wide = pl.BlockSpec((BLK, cols), lambda i: (i, 0))
    half = pl.BlockSpec((BLK, cols // 2), lambda i: (i, 0))
    slab = pl.BlockSpec((2, BLK, 512), lambda i: (i, 0, 0))
    line = pl.BlockSpec((1, 1, cols), lambda i: (i, 0, 0))
    return kernel_call(
        feedback_kernel,
        (groups,),
        [SMEM, line, wide, wide, half, half, half, half],
        [wide, slab, slab],
        [
            jax.ShapeDtypeStruct((rows, cols), BF16),
            jax.ShapeDtypeStruct((2 * groups, BLK, 512), F32),
            jax.ShapeDtypeStruct((2 * groups, BLK, 512), BF16),
        ],
        8 * rows * cols,
    )(c, mask, feedback, own, got_a, got_b, next_a, next_b)


def owner_kernel(yh_ref, mine_ref, peer_ref, moment_ref, new_ref, step_ref):
    mean = (mine_ref[...] + peer_ref[...]) * (1.0 / NODES)
    moment = DECAY * moment_ref[...] + mean
    step = (mean + DECAY * moment).astype(BF16)
    for z in range(8):
        step_ref[z] = step
    own = jnp.where(yh_ref[0] == 0, moment[:, :256], moment[:, 256:])
    for b in range(4):
        new_ref[b] = own[:, b * BLK : (b + 1) * BLK]


def owner_update(yh, mine, peer, moment):
    whole = pl.BlockSpec(memory_space=pltpu.VMEM)
    return kernel_call(
        owner_kernel,
        (),
        [SMEM, whole, whole, whole],
        [whole, whole],
        [
            jax.ShapeDtypeStruct((4, BLK, BLK), F32),
            jax.ShapeDtypeStruct((8, BLK, 512), BF16),
        ],
        8 * BLK * 512,
    )(yh, mine, peer, moment)


def assemble_kernel(c_ref, mine_ref, other_ref, out_ref):
    first = c_ref[0] == 0
    for h in range(2):
        for yh in range(2):
            place = slice(yh * 256, yh * 256 + 256)
            mine, other = mine_ref[h, :, place], other_ref[h, :, place]
            at = h * 1024 + yh * 512
            out_ref[:, at : at + 256] = jnp.where(first, mine, other)
            out_ref[:, at + 256 : at + 512] = jnp.where(first, other, mine)


def assemble(c, mine, other, rows, cols):
    slab = pl.BlockSpec((2, BLK, 512), lambda i: (i, 0, 0))
    return kernel_call(
        assemble_kernel,
        (rows // BLK,),
        [SMEM, slab, slab],
        pl.BlockSpec((BLK, cols), lambda i: (i, 0)),
        jax.ShapeDtypeStruct((rows, cols), BF16),
        4 * rows * cols,
    )(c, mine, other)


def partial_sums(hidden, cotangent, mask, early):
    d = lax.axis_index("dp")
    copies = jnp.broadcast_to(hidden[None], (4, *hidden.shape))
    whole = lax.all_to_all(copies, "t", 0, 0, tiled=True)

    def part(flip, cols):
        rows = lax.dynamic_index_in_dim(whole, d ^ flip, 0, keepdims=False)
        return lax.dot_general(
            rows, cols, (((0,), (0,)), ((), ())), preferred_element_type=F32
        ).astype(BF16)

    def plus(kept, got):
        return (kept.astype(F32) + got.astype(F32)).astype(BF16)

    half = cotangent.shape[1] // 2
    a, b = cotangent[:, :half], cotangent[:, half:]
    far_a, far_b = swap(part(2, a), "dp", 1, 4), swap(part(2, b), "dp", 3, 4)
    got_a, got_b = swap(part(1, a), "dp", 1, 4), swap(part(3, b), "dp", 3, 4)
    kept_a, kept_b, own = part(3, a), part(1, b), part(0, cotangent)
    far_a, kept_a, kept_b, own, mask = lax.optimization_barrier((far_a, kept_a, kept_b, own, mask))
    next_a = swap(plus(kept_a, far_a), "dp", 3, 4)
    next_b = swap(plus(kept_b, far_b), "dp", 1, 4)
    got_a, got_b, early = lax.optimization_barrier((got_a, got_b, early))
    return early, mask, own, got_a, got_b, next_a, next_b


def as_matrix(blocks):
    return blocks.transpose(1, 0, 2).reshape(BLK, -1)


def local(hidden, cotangent, feedback, chosen, momentum):
    rows, cols = feedback.shape[1:]
    rows_blk, cols_blk = rows // BLK, cols // BLK
    c, yh = lax.axis_index("c"), lax.axis_index("yh")
    at_c, at_yh = c.astype(jnp.int32).reshape(1), yh.astype(jnp.int32).reshape(1)
    block_of = (
        jnp.arange(rows_blk, dtype=jnp.int32)[:, None] * cols_blk
        + jnp.arange(cols, dtype=jnp.int32)[None, :] // BLK
    )
    mask = jnp.any(chosen.reshape(-1, 1, 1) == block_of[None], axis=0).astype(F32)
    moment = as_matrix(momentum[0, 0])
    far_moment = swap(moment, "yh", 1, 2)
    far_moment, mask, *parts = partial_sums(hidden, cotangent, mask[:, None], far_moment)
    moment = jnp.where(
        yh == 0, jnp.concatenate([moment, far_moment], 1), jnp.concatenate([far_moment, moment], 1)
    )
    feedback_new, mine, other = error_feedback(at_c, mask, feedback[0], *parts)
    pair = (mine + swap(other, "c", 1, 2).astype(F32)).astype(BF16)
    got = lax.all_to_all(pair, "z", 0, 0, tiled=True)
    near = jnp.sum(got.astype(F32), axis=0)
    momentum_new, copies = owner_update(at_yh, near, swap(near, "yh", 1, 2), moment)
    every = lax.all_to_all(copies, "z", 0, 0, tiled=True)
    step = assemble(at_c, every, swap(every, "c", 1, 2), rows, cols)
    return feedback_new[None], momentum_new[None, None], step


def solution(mesh):
    fine = Mesh(mesh.devices.reshape(SHAPE), (*NODE, "dp", "t"))
    tokens = P((*NODE, "dp"), "t")
    return jax.shard_map(
        local,
        mesh=fine,
        in_specs=(
            tokens,
            tokens,
            P(NODE, "dp", "t"),
            P(NODE, "dp", "t", None),
            P("dp", "t", NODE, None, None),
        ),
        out_specs=(P(NODE, "dp", "t"), P("dp", "t", NODE, None, None), P("dp", "t")),
        check_vma=False,
    )
```

```python
import jax
import jax.numpy as jnp
from jax import lax
from jax.experimental import pallas as pl
from jax.experimental.pallas import tpu as pltpu
from jax.sharding import Mesh, PartitionSpec as P

BLK = 64
DECAY = 0.9
NODES = 32
F32, BF16 = jnp.float32, jnp.bfloat16
NODE = ("z", "yh", "c")
SHAPE = (8, 2, 2, 4, 4)
VMEM_LIMIT = 32 * 1024 * 1024


def swap(value, axis, flip, size):
    return lax.ppermute(value, axis, [(i, i ^ flip) for i in range(size)])


def kernel_call(body, grid, ins, outs, out_shape, cost):
    return pl.pallas_call(
        body,
        grid=grid,
        in_specs=ins,
        out_specs=outs,
        out_shape=out_shape,
        compiler_params=pltpu.CompilerParams(vmem_limit_bytes=VMEM_LIMIT),
        cost_estimate=pl.CostEstimate(flops=cost, bytes_accessed=cost, transcendentals=0),
    )


SMEM = pl.BlockSpec(memory_space=pltpu.SMEM)


def feedback_kernel(
    c_ref, mask_ref, fb_ref, own_ref, got_a, got_b, next_a, next_b, new_ref, mine_ref, other_ref
):
    first = c_ref[0] == 0
    for h, got, nxt in ((0, got_a, next_a), (1, got_b, next_b)):
        for yh in range(2):
            sent = []
            for c in range(2):
                near = slice(yh * 512 + c * 256, yh * 512 + c * 256 + 256)
                far = slice(h * 1024 + near.start, h * 1024 + near.stop)
                acc = (
                    own_ref[:, far].astype(F32)
                    + got[:, near].astype(F32)
                    + nxt[:, near].astype(F32)
                )
                acc = fb_ref[:, far].astype(F32) + acc
                chosen = jnp.broadcast_to(mask_ref[0, :, far], acc.shape) > 0.5
                new_ref[:, far] = jnp.where(chosen, 0.0, acc).astype(BF16)
                sent.append(jnp.where(chosen, acc, 0.0))
            place = slice(yh * 256, yh * 256 + 256)
            mine_ref[h, :, place] = jnp.where(first, sent[0], sent[1])
            other_ref[h, :, place] = jnp.where(first, sent[1], sent[0]).astype(BF16)


def error_feedback(c, mask, feedback, own, got_a, got_b, next_a, next_b):
    rows, cols = feedback.shape
    groups = rows // BLK
    wide = pl.BlockSpec((BLK, cols), lambda i: (i, 0))
    half = pl.BlockSpec((BLK, cols // 2), lambda i: (i, 0))
    slab = pl.BlockSpec((2, BLK, 512), lambda i: (i, 0, 0))
    line = pl.BlockSpec((1, 1, cols), lambda i: (i, 0, 0))
    return kernel_call(
        feedback_kernel,
        (groups,),
        [SMEM, line, wide, wide, half, half, half, half],
        [wide, slab, slab],
        [
            jax.ShapeDtypeStruct((rows, cols), BF16),
            jax.ShapeDtypeStruct((2 * groups, BLK, 512), F32),
            jax.ShapeDtypeStruct((2 * groups, BLK, 512), BF16),
        ],
        8 * rows * cols,
    )(c, mask, feedback, own, got_a, got_b, next_a, next_b)


def owner_kernel(yh_ref, mine_ref, peer_ref, moment_ref, new_ref, step_ref):
    mean = (mine_ref[...] + peer_ref[...]) * (1.0 / NODES)
    moment = DECAY * moment_ref[...] + mean
    step = (mean + DECAY * moment).astype(BF16)
    for z in range(8):
        step_ref[z] = step
    own = jnp.where(yh_ref[0] == 0, moment[:, :256], moment[:, 256:])
    for b in range(4):
        new_ref[b] = own[:, b * BLK : (b + 1) * BLK]


def owner_update(yh, mine, peer, moment):
    whole = pl.BlockSpec(memory_space=pltpu.VMEM)
    return kernel_call(
        owner_kernel,
        (),
        [SMEM, whole, whole, whole],
        [whole, whole],
        [
            jax.ShapeDtypeStruct((4, BLK, BLK), F32),
            jax.ShapeDtypeStruct((8, BLK, 512), BF16),
        ],
        8 * BLK * 512,
    )(yh, mine, peer, moment)


def assemble_kernel(c_ref, mine_ref, other_ref, out_ref):
    first = c_ref[0] == 0
    for h in range(2):
        for yh in range(2):
            place = slice(yh * 256, yh * 256 + 256)
            mine, other = mine_ref[h, :, place], other_ref[h, :, place]
            at = h * 1024 + yh * 512
            out_ref[:, at : at + 256] = jnp.where(first, mine, other)
            out_ref[:, at + 256 : at + 512] = jnp.where(first, other, mine)


def assemble(c, mine, other, rows, cols):
    slab = pl.BlockSpec((2, BLK, 512), lambda i: (i, 0, 0))
    return kernel_call(
        assemble_kernel,
        (rows // BLK,),
        [SMEM, slab, slab],
        pl.BlockSpec((BLK, cols), lambda i: (i, 0)),
        jax.ShapeDtypeStruct((rows, cols), BF16),
        4 * rows * cols,
    )(c, mine, other)


def partial_sums(hidden, cotangent, mask, early):
    d, t = lax.axis_index("dp"), lax.axis_index("t")
    far = swap(hidden, "t", 2, 4)
    near = swap(hidden, "t", 1, 4)
    whole = lax.optimization_barrier((hidden, near, far, swap(far, "t", 1, 4), early))
    early = whole[4]
    whole = jnp.stack(whole[:4])

    def part(flip, cols, shards=whole):
        rows = lax.dynamic_index_in_dim(shards, t ^ d ^ flip, 0, keepdims=False)
        return lax.dot_general(
            rows, cols, (((0,), (0,)), ((), ())), preferred_element_type=F32
        ).astype(BF16)

    def plus(kept, got):
        return (kept.astype(F32) + got.astype(F32)).astype(BF16)

    half = cotangent.shape[1] // 2
    a, b = cotangent[:, :half], cotangent[:, half:]
    give_a, give_b = part(2, a), part(2, b)
    far_a, far_b = swap(give_a, "dp", 1, 4), swap(give_b, "dp", 3, 4)
    later, give_a, give_b = lax.optimization_barrier((whole, give_a, give_b))
    got_a, got_b = swap(part(1, a, later), "dp", 1, 4), swap(part(3, b, later), "dp", 3, 4)
    kept_a, kept_b, own = part(3, a, later), part(1, b, later), part(0, cotangent, later)
    far_a, kept_a, kept_b, own, mask = lax.optimization_barrier((far_a, kept_a, kept_b, own, mask))
    next_a = swap(plus(kept_a, far_a), "dp", 3, 4)
    next_b = swap(plus(kept_b, far_b), "dp", 1, 4)
    return early, mask, own, got_a, got_b, next_a, next_b


def as_matrix(blocks):
    return blocks.transpose(1, 0, 2).reshape(BLK, -1)


def local(hidden, cotangent, feedback, chosen, momentum):
    rows, cols = feedback.shape[1:]
    rows_blk, cols_blk = rows // BLK, cols // BLK
    c, yh = lax.axis_index("c"), lax.axis_index("yh")
    at_c, at_yh = c.astype(jnp.int32).reshape(1), yh.astype(jnp.int32).reshape(1)
    block_of = (
        jnp.arange(rows_blk, dtype=jnp.int32)[:, None] * cols_blk
        + jnp.arange(cols, dtype=jnp.int32)[None, :] // BLK
    )
    mask = jnp.any(chosen.reshape(-1, 1, 1) == block_of[None], axis=0).astype(F32)
    moment = as_matrix(momentum[0, 0])
    far_moment = swap(moment, "yh", 1, 2)
    far_moment, mask, *parts = partial_sums(hidden, cotangent, mask[:, None], far_moment)
    moment = jnp.where(
        yh == 0, jnp.concatenate([moment, far_moment], 1), jnp.concatenate([far_moment, moment], 1)
    )
    feedback_new, mine, other = error_feedback(at_c, mask, feedback[0], *parts)
    pair = (mine + swap(other, "c", 1, 2).astype(F32)).astype(BF16)
    got = lax.all_to_all(pair, "z", 0, 0, tiled=True)
    near = jnp.sum(got.astype(F32), axis=0)
    momentum_new, copies = owner_update(at_yh, near, swap(near, "yh", 1, 2), moment)
    every = lax.all_to_all(copies, "z", 0, 0, tiled=True)
    step = assemble(at_c, every, swap(every, "c", 1, 2), rows, cols)
    return feedback_new[None], momentum_new[None, None], step


def solution(mesh):
    fine = Mesh(mesh.devices.reshape(SHAPE), (*NODE, "dp", "t"))
    tokens = P((*NODE, "dp"), "t")
    return jax.shard_map(
        local,
        mesh=fine,
        in_specs=(
            tokens,
            tokens,
            P(NODE, "dp", "t"),
            P(NODE, "dp", "t", None),
            P("dp", "t", NODE, None, None),
        ),
        out_specs=(P(NODE, "dp", "t"), P("dp", "t", NODE, None, None), P("dp", "t")),
        check_vma=False,
    )
```

```python
import functools

import jax
import jax.numpy as jnp
from jax import lax
from jax.experimental import pallas as pl
from jax.experimental.pallas import tpu as pltpu
from jax.sharding import Mesh, PartitionSpec as P

BLK = 64
LANES = 128
DECAY = 0.9
NODES = 32
F32, BF16 = jnp.float32, jnp.bfloat16
NODE = ("z", "yh", "c")
SHAPE = (8, 2, 2, 4, 4)
VMEM_LIMIT = 32 * 1024 * 1024


def swap(value, axis, flip, size):
    return lax.ppermute(value, axis, [(i, i ^ flip) for i in range(size)])


def kernel_call(body, grid, ins, outs, out_shape, cost):
    return pl.pallas_call(
        body,
        grid=grid,
        in_specs=ins,
        out_specs=outs,
        out_shape=out_shape,
        compiler_params=pltpu.CompilerParams(vmem_limit_bytes=VMEM_LIMIT),
        cost_estimate=pl.CostEstimate(flops=cost, bytes_accessed=cost, transcendentals=0),
    )


SMEM = pl.BlockSpec(memory_space=pltpu.SMEM)


def place_of(block):
    row, col = block // 32, block % 32
    rows = pl.ds(pl.multiple_of(row * BLK, BLK), BLK)
    return rows, pl.ds(pl.multiple_of(col // 2 * LANES, LANES), LANES), col % 2


def lane_halves():
    return lax.broadcasted_iota(jnp.int32, (BLK, LANES), 1) // BLK


def pack_kernel(picks, base, pieces, list_ref, *refs):
    mats, outs = refs[: len(picks)], refs[len(picks) :]
    upper = lane_halves() == 1
    span = 64 // 2 // pieces
    for n, k in enumerate(picks):
        for p in range(pieces):
            out_ref = outs[n * pieces + p]

            def tile(q, carry, k=k, n=n, p=p, out_ref=out_ref):
                slot = base + 2 * (p * span + q)
                sides = []
                for side in range(2):
                    rows, cols, half = place_of(list_ref[k, slot + side])
                    block = mats[n][rows, cols].astype(F32)
                    sides.append(pltpu.roll(block, (half + side) % 2 * BLK, 1))
                at = pl.ds(pl.multiple_of(q * LANES, LANES), LANES)
                out_ref[:, at] = jnp.where(upper, sides[1], sides[0]).astype(BF16)
                return carry

            lax.fori_loop(0, span, tile, 0, unroll=4)


def pack(lists, mats, picks, base, pieces):
    whole = pl.BlockSpec(memory_space=pltpu.VMEM)
    count = len(picks) * pieces
    return kernel_call(
        functools.partial(pack_kernel, picks, base, pieces),
        (),
        [SMEM] + [whole] * len(picks),
        [whole] * count,
        [jax.ShapeDtypeStruct((BLK, 64 * BLK // pieces), BF16)] * count,
        1 << 20,
    )(lists, *mats)


def unpack(list_ref, base, pieces, grad_ref):
    halves = lane_halves()
    span = 64 // 2 // len(pieces)
    for p, terms in enumerate(pieces):

        def tile(q, carry, p=p, terms=terms):
            at = pl.ds(pl.multiple_of(q * LANES, LANES), LANES)
            value = terms[0][:, at].astype(F32)
            for term in terms[1:]:
                value = value + term[:, at].astype(F32)
            for side in range(2):
                rows, cols, half = place_of(list_ref[0, base + 2 * (p * span + q) + side])
                moved = pltpu.roll(value, (half + side) % 2 * BLK, 1)
                grad_ref[rows, cols] = jnp.where(halves == half, moved, grad_ref[rows, cols])
            return carry

        lax.fori_loop(0, span, tile, 0, unroll=2)


def chosen_kernel(
    list_ref, c_ref, mask_ref, fb_ref, own_ref, got_a, got_b, next_a, next_b, mine_ref, other_ref, grad_ref
):
    row = pl.program_id(0)

    @pl.when(row == 0)
    def _():
        unpack(list_ref, 0, ((got_a, next_a), (got_b, next_b)), grad_ref)

    first = c_ref[0] == 0
    rows = pl.ds(pl.multiple_of(row * BLK, BLK), BLK)
    for h in range(2):
        for yh in range(2):
            sent = []
            for c in range(2):
                at = h * 1024 + yh * 512 + c * 256
                at = slice(at, at + 256)
                acc = own_ref[:, at].astype(F32) + grad_ref[rows, at]
                acc = fb_ref[:, at].astype(F32) + acc
                chosen = jnp.broadcast_to(mask_ref[0, :, at], acc.shape) > 0.5
                sent.append(jnp.where(chosen, acc, 0.0))
            place = slice(yh * 256, yh * 256 + 256)
            mine_ref[h, :, place] = jnp.where(first, sent[0], sent[1])
            other_ref[h, :, place] = jnp.where(first, sent[1], sent[0]).astype(BF16)


def residual_kernel(list_ref, mask_ref, fb_ref, own_ref, got_1, got_2, got_3, new_ref, grad_ref):
    row = pl.program_id(0)

    @pl.when(row == 0)
    def _():
        unpack(list_ref, 64, ((got_1, got_2, got_3),), grad_ref)

    rows = pl.ds(pl.multiple_of(row * BLK, BLK), BLK)
    for at in range(0, fb_ref.shape[1], 256):
        at = slice(at, at + 256)
        acc = own_ref[:, at].astype(F32) + grad_ref[rows, at]
        acc = fb_ref[:, at].astype(F32) + acc
        chosen = jnp.broadcast_to(mask_ref[0, :, at], acc.shape) > 0.5
        new_ref[:, at] = jnp.where(chosen, 0.0, acc).astype(BF16)


def state_call(body, scalars, mask, feedback, own, received, outs, out_shape):
    rows, cols = feedback.shape
    wide = pl.BlockSpec((BLK, cols), lambda i: (i, 0))
    line = pl.BlockSpec((1, 1, cols), lambda i: (i, 0, 0))
    packed = [pl.BlockSpec(r.shape, lambda i: (0, 0)) for r in received]
    return pl.pallas_call(
        body,
        grid=(rows // BLK,),
        in_specs=[SMEM] * len(scalars) + [line, wide, wide] + packed,
        out_specs=outs,
        out_shape=out_shape,
        scratch_shapes=[pltpu.VMEM((rows, cols), F32)],
        compiler_params=pltpu.CompilerParams(vmem_limit_bytes=VMEM_LIMIT),
        cost_estimate=pl.CostEstimate(flops=1 << 22, bytes_accessed=1 << 22, transcendentals=0),
    )(*scalars, mask, feedback, own, *received)


def chosen_sums(lists, c, mask, feedback, own, *received):
    slab = pl.BlockSpec((2, BLK, 512), lambda i: (i, 0, 0))
    shape = (8, BLK, 512)
    return state_call(
        chosen_kernel, (lists, c), mask, feedback, own, received, [slab, slab],
        [jax.ShapeDtypeStruct(shape, F32), jax.ShapeDtypeStruct(shape, BF16)],
    )


def residual(lists, mask, feedback, own, *received):
    rows, cols = feedback.shape
    return state_call(
        residual_kernel, (lists,), mask, feedback, own, received,
        pl.BlockSpec((BLK, cols), lambda i: (i, 0)), jax.ShapeDtypeStruct((rows, cols), BF16),
    )


def owner_kernel(yh_ref, mine_ref, peer_ref, moment_ref, new_ref, step_ref):
    mean = (mine_ref[...] + peer_ref[...]) * (1.0 / NODES)
    moment = DECAY * moment_ref[...] + mean
    step = (mean + DECAY * moment).astype(BF16)
    for z in range(8):
        step_ref[z] = step
    own = jnp.where(yh_ref[0] == 0, moment[:, :256], moment[:, 256:])
    for b in range(4):
        new_ref[b] = own[:, b * BLK : (b + 1) * BLK]


def owner_update(yh, mine, peer, moment):
    whole = pl.BlockSpec(memory_space=pltpu.VMEM)
    return kernel_call(
        owner_kernel,
        (),
        [SMEM, whole, whole, whole],
        [whole, whole],
        [
            jax.ShapeDtypeStruct((4, BLK, BLK), F32),
            jax.ShapeDtypeStruct((8, BLK, 512), BF16),
        ],
        8 * BLK * 512,
    )(yh, mine, peer, moment)


def assemble_kernel(c_ref, mine_ref, other_ref, out_ref):
    first = c_ref[0] == 0
    for h in range(2):
        for yh in range(2):
            place = slice(yh * 256, yh * 256 + 256)
            mine, other = mine_ref[h, :, place], other_ref[h, :, place]
            at = h * 1024 + yh * 512
            out_ref[:, at : at + 256] = jnp.where(first, mine, other)
            out_ref[:, at + 256 : at + 512] = jnp.where(first, other, mine)


def assemble(c, mine, other, rows, cols):
    slab = pl.BlockSpec((2, BLK, 512), lambda i: (i, 0, 0))
    return kernel_call(
        assemble_kernel,
        (rows // BLK,),
        [SMEM, slab, slab],
        pl.BlockSpec((BLK, cols), lambda i: (i, 0)),
        jax.ShapeDtypeStruct((rows, cols), BF16),
        4 * rows * cols,
    )(c, mine, other)


def block_lists(chosen, count):
    near = swap(chosen, "dp", 1, 4)
    across = swap(jnp.stack([chosen, near]), "dp", 3, 4)
    lists = jnp.stack([chosen, near, across[1], across[0]])
    blocks = jnp.arange(count, dtype=jnp.int32)
    left = jnp.all(lists[:, :, None] != blocks, axis=1)
    before = blocks[:, None] < blocks[None, :]
    rank = jnp.sum(jnp.where(left[:, :, None] & before, 1, 0), axis=1)
    slots = jnp.arange(count // 2, dtype=jnp.int32)
    hit = left[:, None, :] & (rank[:, None, :] == slots[None, :, None])
    others = jnp.sum(jnp.where(hit, blocks, 0), axis=2)
    return jnp.concatenate([lists, others], axis=1)


def gather_hidden(hidden):
    far = swap(hidden, "t", 2, 4)
    near = swap(hidden, "t", 1, 4)
    return hidden, near, far, swap(far, "t", 1, 4)


def plus(kept, got):
    return (kept.astype(F32) + got.astype(F32)).astype(BF16)


def as_matrix(blocks):
    return blocks.transpose(1, 0, 2).reshape(BLK, -1)


def local(hidden, cotangent, feedback, chosen, momentum):
    rows, cols = feedback.shape[1:]
    rows_blk, cols_blk = rows // BLK, cols // BLK
    c, yh = lax.axis_index("c"), lax.axis_index("yh")
    at_c, at_yh = c.astype(jnp.int32).reshape(1), yh.astype(jnp.int32).reshape(1)
    block_of = (
        jnp.arange(rows_blk, dtype=jnp.int32)[:, None] * cols_blk
        + jnp.arange(cols, dtype=jnp.int32)[None, :] // BLK
    )
    mask = jnp.any(chosen.reshape(-1, 1, 1) == block_of[None], axis=0).astype(F32)
    moment = as_matrix(momentum[0, 0])
    far_moment = swap(moment, "yh", 1, 2)
    mask = mask[:, None]
    lists = block_lists(chosen.reshape(-1), rows_blk * cols_blk)
    *shards, far_moment, lists = lax.optimization_barrier(
        (*gather_hidden(hidden), far_moment, lists)
    )
    shards = jnp.stack(shards)
    moment = jnp.where(
        yh == 0, jnp.concatenate([moment, far_moment], 1), jnp.concatenate([far_moment, moment], 1)
    )
    d, t = lax.axis_index("dp"), lax.axis_index("t")

    def product(flip, shards):
        part = lax.dynamic_index_in_dim(shards, t ^ d ^ flip, 0, keepdims=False)
        return lax.dot_general(
            part, cotangent, (((0,), (0,)), ((), ())), preferred_element_type=F32
        ).astype(BF16)

    far_rows = product(2, shards)
    give_a, give_b = pack(lists, (far_rows,), (2,), 0, 2)
    far_a, far_b = swap(give_a, "dp", 1, 4), swap(give_b, "dp", 3, 4)
    shards, give_a, give_b = lax.optimization_barrier((shards, give_a, give_b))
    near_rows, side_rows = product(1, shards), product(3, shards)
    near_a, near_b, side_a, side_b = pack(lists, (near_rows, side_rows), (1, 3), 0, 2)
    got_a, got_b = swap(near_a, "dp", 1, 4), swap(side_b, "dp", 3, 4)
    own = product(0, shards)
    far_a, near_b, side_a, own, mask = lax.optimization_barrier((far_a, near_b, side_a, own, mask))
    next_a = swap(plus(side_a, far_a), "dp", 3, 4)
    next_b = swap(plus(near_b, far_b), "dp", 1, 4)
    mine, other = chosen_sums(
        lists, at_c, mask, feedback[0], own, got_a, got_b, next_a, next_b
    )
    pair = (mine + swap(other, "c", 1, 2).astype(F32)).astype(BF16)
    near_rows, far_rows, side_rows, _ = lax.optimization_barrier(
        (near_rows, far_rows, side_rows, pair)
    )
    left = pack(lists, (near_rows, far_rows, side_rows), (1, 2, 3), 64, 1)
    left = [swap(part, "dp", flip, 4) for flip, part in zip((1, 2, 3), left)]
    got = lax.all_to_all(pair, "z", 0, 0, tiled=True)
    near = jnp.sum(got.astype(F32), axis=0)
    momentum_new, copies = owner_update(at_yh, near, swap(near, "yh", 1, 2), moment)
    every = lax.all_to_all(copies, "z", 0, 0, tiled=True)
    *left, _ = lax.optimization_barrier((*left, copies))
    feedback_new = residual(lists, mask, feedback[0], own, *left)
    step = assemble(at_c, every, swap(every, "c", 1, 2), rows, cols)
    return feedback_new[None], momentum_new[None, None], step


def solution(mesh):
    fine = Mesh(mesh.devices.reshape(SHAPE), (*NODE, "dp", "t"))
    tokens = P((*NODE, "dp"), "t")
    return jax.shard_map(
        local,
        mesh=fine,
        in_specs=(
            tokens,
            tokens,
            P(NODE, "dp", "t"),
            P(NODE, "dp", "t", None),
            P("dp", "t", NODE, None, None),
        ),
        out_specs=(P(NODE, "dp", "t"), P("dp", "t", NODE, None, None), P("dp", "t")),
        check_vma=False,
    )
```

```python
import functools

import jax
import jax.numpy as jnp
from jax import lax
from jax.experimental import pallas as pl
from jax.experimental.pallas import tpu as pltpu
from jax.sharding import Mesh, PartitionSpec as P

BLK = 64
LANES = 128
HALF = 64
DECAY = 0.9
NODES = 32
F32, BF16 = jnp.float32, jnp.bfloat16
NODE = ("z", "yh", "c")
SHAPE = (8, 2, 2, 4, 4)
VMEM_LIMIT = 32 * 1024 * 1024


def swap(value, axis, flip, size):
    return lax.ppermute(value, axis, [(i, i ^ flip) for i in range(size)])


def kernel_call(body, grid, ins, outs, out_shape, cost):
    return pl.pallas_call(
        body,
        grid=grid,
        in_specs=ins,
        out_specs=outs,
        out_shape=out_shape,
        compiler_params=pltpu.CompilerParams(vmem_limit_bytes=VMEM_LIMIT),
        cost_estimate=pl.CostEstimate(flops=cost, bytes_accessed=cost, transcendentals=0),
    )


SMEM = pl.BlockSpec(memory_space=pltpu.SMEM)


def place_of(block):
    row, col = block // 32, block % 32
    rows = pl.ds(pl.multiple_of(row * BLK, BLK), BLK)
    return rows, pl.ds(pl.multiple_of(col // 2 * LANES, LANES), LANES), col % 2


def lane_halves():
    return lax.broadcasted_iota(jnp.int32, (BLK, LANES), 1) // BLK


def pack_kernel(k, base, list_ref, mat_ref, out_ref):
    upper = lane_halves() == 1

    def tile(q, carry):
        sides = []
        for side in range(2):
            rows, cols, half = place_of(list_ref[k, base + 2 * q + side])
            block = mat_ref[rows, cols]
            sides.append(jnp.where(half == side, block, pltpu.roll(block, BLK, 1)))
        at = pl.ds(pl.multiple_of(q * LANES, LANES), LANES)
        out_ref[:, at] = jnp.where(upper, sides[1], sides[0])
        return carry

    lax.fori_loop(0, HALF // 2, tile, 0, unroll=True)


def pack(lists, mat, k, base):
    whole = pl.BlockSpec(memory_space=pltpu.VMEM)
    return kernel_call(
        functools.partial(pack_kernel, k, base),
        (),
        [SMEM, whole],
        whole,
        jax.ShapeDtypeStruct((BLK, HALF * BLK), BF16),
        1 << 20,
    )(lists, mat)


def unpack(list_ref, base, terms, grad_ref):
    halves = lane_halves()

    def tile(q, carry):
        at = pl.ds(pl.multiple_of(q * LANES, LANES), LANES)
        value = terms[0][:, at].astype(F32)
        for term in terms[1:]:
            value = value + term[:, at].astype(F32)
        turned = pltpu.roll(value, BLK, 1)
        for side in range(2):
            rows, cols, half = place_of(list_ref[0, base + 2 * q + side])
            moved = jnp.where(half == side, value, turned)
            grad_ref[rows, cols] = jnp.where(halves == half, moved, grad_ref[rows, cols])
        return carry

    lax.fori_loop(0, HALF // 2, tile, 0, unroll=True)


def chosen_kernel(
    list_ref, c_ref, mask_ref, fb_ref, own_ref, got_1, got_2, got_3, mine_ref, other_ref, grad_ref
):
    row = pl.program_id(0)

    @pl.when(row == 0)
    def _():
        unpack(list_ref, 0, (got_1, got_2, got_3), grad_ref)

    first = c_ref[0] == 0
    rows = pl.ds(pl.multiple_of(row * BLK, BLK), BLK)
    for h in range(2):
        for yh in range(2):
            sent = []
            for c in range(2):
                at = h * 1024 + yh * 512 + c * 256
                at = slice(at, at + 256)
                acc = own_ref[:, at].astype(F32) + grad_ref[rows, at]
                acc = fb_ref[:, at].astype(F32) + acc
                chosen = jnp.broadcast_to(mask_ref[0, :, at], acc.shape) > 0.5
                sent.append(jnp.where(chosen, acc, 0.0))
            place = slice(yh * 256, yh * 256 + 256)
            mine_ref[h, :, place] = jnp.where(first, sent[0], sent[1])
            other_ref[h, :, place] = jnp.where(first, sent[1], sent[0]).astype(BF16)


def residual_kernel(list_ref, mask_ref, fb_ref, own_ref, got_1, got_2, got_3, new_ref, grad_ref):
    row = pl.program_id(0)

    @pl.when(row == 0)
    def _():
        unpack(list_ref, HALF, (got_1, got_2, got_3), grad_ref)

    rows = pl.ds(pl.multiple_of(row * BLK, BLK), BLK)
    for at in range(0, fb_ref.shape[1], 256):
        at = slice(at, at + 256)
        acc = own_ref[:, at].astype(F32) + grad_ref[rows, at]
        acc = fb_ref[:, at].astype(F32) + acc
        chosen = jnp.broadcast_to(mask_ref[0, :, at], acc.shape) > 0.5
        new_ref[:, at] = jnp.where(chosen, 0.0, acc).astype(BF16)


def state_call(body, scalars, mask, feedback, own, received, outs, out_shape):
    rows, cols = feedback.shape
    wide = pl.BlockSpec((BLK, cols), lambda i: (i, 0))
    line = pl.BlockSpec((1, 1, cols), lambda i: (i, 0, 0))
    packed = [pl.BlockSpec(r.shape, lambda i: (0, 0)) for r in received]
    return pl.pallas_call(
        body,
        grid=(rows // BLK,),
        in_specs=[SMEM] * len(scalars) + [line, wide, wide] + packed,
        out_specs=outs,
        out_shape=out_shape,
        scratch_shapes=[pltpu.VMEM((rows, cols), F32)],
        compiler_params=pltpu.CompilerParams(vmem_limit_bytes=VMEM_LIMIT),
        cost_estimate=pl.CostEstimate(flops=1 << 22, bytes_accessed=1 << 22, transcendentals=0),
    )(*scalars, mask, feedback, own, *received)


def chosen_sums(lists, c, mask, feedback, own, *received):
    slab = pl.BlockSpec((2, BLK, 512), lambda i: (i, 0, 0))
    shape = (8, BLK, 512)
    return state_call(
        chosen_kernel, (lists, c), mask, feedback, own, received, [slab, slab],
        [jax.ShapeDtypeStruct(shape, F32), jax.ShapeDtypeStruct(shape, BF16)],
    )


def residual(lists, mask, feedback, own, *received):
    rows, cols = feedback.shape
    return state_call(
        residual_kernel, (lists,), mask, feedback, own, received,
        pl.BlockSpec((BLK, cols), lambda i: (i, 0)), jax.ShapeDtypeStruct((rows, cols), BF16),
    )


def owner_kernel(yh_ref, mine_ref, peer_ref, moment_ref, new_ref, step_ref):
    mean = (mine_ref[...] + peer_ref[...]) * (1.0 / NODES)
    moment = DECAY * moment_ref[...] + mean
    step = (mean + DECAY * moment).astype(BF16)
    for z in range(8):
        step_ref[z] = step
    own = jnp.where(yh_ref[0] == 0, moment[:, :256], moment[:, 256:])
    for b in range(4):
        new_ref[b] = own[:, b * BLK : (b + 1) * BLK]


def owner_update(yh, mine, peer, moment):
    whole = pl.BlockSpec(memory_space=pltpu.VMEM)
    return kernel_call(
        owner_kernel,
        (),
        [SMEM, whole, whole, whole],
        [whole, whole],
        [
            jax.ShapeDtypeStruct((4, BLK, BLK), F32),
            jax.ShapeDtypeStruct((8, BLK, 512), BF16),
        ],
        8 * BLK * 512,
    )(yh, mine, peer, moment)


def assemble_kernel(c_ref, mine_ref, other_ref, out_ref):
    first = c_ref[0] == 0
    for h in range(2):
        for yh in range(2):
            place = slice(yh * 256, yh * 256 + 256)
            mine, other = mine_ref[h, :, place], other_ref[h, :, place]
            at = h * 1024 + yh * 512
            out_ref[:, at : at + 256] = jnp.where(first, mine, other)
            out_ref[:, at + 256 : at + 512] = jnp.where(first, other, mine)


def assemble(c, mine, other, rows, cols):
    slab = pl.BlockSpec((2, BLK, 512), lambda i: (i, 0, 0))
    return kernel_call(
        assemble_kernel,
        (rows // BLK,),
        [SMEM, slab, slab],
        pl.BlockSpec((BLK, cols), lambda i: (i, 0)),
        jax.ShapeDtypeStruct((rows, cols), BF16),
        4 * rows * cols,
    )(c, mine, other)


def block_lists(chosen, count):
    near = swap(chosen, "dp", 1, 4)
    across = swap(jnp.stack([chosen, near]), "dp", 3, 4)
    lists = jnp.stack([chosen, near, across[1], across[0]])
    blocks = jnp.arange(count, dtype=jnp.int32)
    left = jnp.all(lists[:, :, None] != blocks, axis=1)
    before = blocks[:, None] < blocks[None, :]
    rank = jnp.sum(jnp.where(left[:, :, None] & before, 1, 0), axis=1)
    slots = jnp.arange(count // 2, dtype=jnp.int32)
    hit = left[:, None, :] & (rank[:, None, :] == slots[None, :, None])
    others = jnp.sum(jnp.where(hit, blocks, 0), axis=2)
    return jnp.concatenate([lists, others], axis=1)


def gather_hidden(hidden):
    far = swap(hidden, "t", 2, 4)
    near = swap(hidden, "t", 1, 4)
    return hidden, near, far, swap(far, "t", 1, 4)


def as_matrix(blocks):
    return blocks.transpose(1, 0, 2).reshape(BLK, -1)


def local(hidden, cotangent, feedback, chosen, momentum):
    rows, cols = feedback.shape[1:]
    rows_blk, cols_blk = rows // BLK, cols // BLK
    c, yh = lax.axis_index("c"), lax.axis_index("yh")
    at_c, at_yh = c.astype(jnp.int32).reshape(1), yh.astype(jnp.int32).reshape(1)
    block_of = (
        jnp.arange(rows_blk, dtype=jnp.int32)[:, None] * cols_blk
        + jnp.arange(cols, dtype=jnp.int32)[None, :] // BLK
    )
    mask = jnp.any(chosen.reshape(-1, 1, 1) == block_of[None], axis=0).astype(F32)
    moment = as_matrix(momentum[0, 0])
    mask = mask[:, None]
    lists = block_lists(chosen.reshape(-1), rows_blk * cols_blk)
    *shards, lists = lax.optimization_barrier((*gather_hidden(hidden), lists))
    shards = jnp.stack(shards)
    d, t = lax.axis_index("dp"), lax.axis_index("t")

    def product(flip, shards):
        part = lax.dynamic_index_in_dim(shards, t ^ d ^ flip, 0, keepdims=False)
        return lax.dot_general(
            part, cotangent, (((0,), (0,)), ((), ())), preferred_element_type=F32
        ).astype(BF16)

    parts, got = {}, {}
    for k in (2, 1, 3):
        parts[k] = product(k, shards)
        given = pack(lists, parts[k], k, 0)
        got[k] = swap(given, "dp", k, 4)
        shards, given = lax.optimization_barrier((shards, given))
    moment, given = lax.optimization_barrier((moment, given))
    far_moment = swap(moment, "yh", 1, 2)
    own = product(0, shards)
    left = [pack(lists, parts[k], k, HALF) for k in (1, 2, 3)]
    got = [got[k] for k in (1, 2, 3)]
    *got, far_moment, own, left_1, left_2, left_3 = lax.optimization_barrier(
        (*got, far_moment, own, *left)
    )
    mine, other = chosen_sums(lists, at_c, mask, feedback[0], own, *got)
    pair = (mine + swap(other, "c", 1, 2).astype(F32)).astype(BF16)
    pair, *left = lax.optimization_barrier((pair, left_1, left_2, left_3))
    left = [swap(part, "dp", k, 4) for k, part in zip((1, 2, 3), left)]
    across = lax.all_to_all(pair, "z", 0, 0, tiled=True)
    near = jnp.sum(across.astype(F32), axis=0)
    far = swap(near, "yh", 1, 2)
    far, *left = lax.optimization_barrier((far, *left))
    moment = jnp.where(
        yh == 0, jnp.concatenate([moment, far_moment], 1), jnp.concatenate([far_moment, moment], 1)
    )
    momentum_new, copies = owner_update(at_yh, near, far, moment)
    every = lax.all_to_all(copies, "z", 0, 0, tiled=True)
    *left, _ = lax.optimization_barrier((*left, copies))
    feedback_new = residual(lists, mask, feedback[0], own, *left)
    step = assemble(at_c, every, swap(every, "c", 1, 2), rows, cols)
    return feedback_new[None], momentum_new[None, None], step


def solution(mesh):
    fine = Mesh(mesh.devices.reshape(SHAPE), (*NODE, "dp", "t"))
    tokens = P((*NODE, "dp"), "t")
    return jax.shard_map(
        local,
        mesh=fine,
        in_specs=(
            tokens,
            tokens,
            P(NODE, "dp", "t"),
            P(NODE, "dp", "t", None),
            P("dp", "t", NODE, None, None),
        ),
        out_specs=(P(NODE, "dp", "t"), P("dp", "t", NODE, None, None), P("dp", "t")),
        check_vma=False,
    )
```

```python
import functools

import jax
import jax.numpy as jnp
from jax import lax
from jax.experimental import pallas as pl
from jax.experimental.pallas import tpu as pltpu
from jax.sharding import Mesh, PartitionSpec as P

BLK = 64
LANES = 128
HALF = 64
DECAY = 0.9
NODES = 32
F32, BF16 = jnp.float32, jnp.bfloat16
NODE = ("z", "yh", "c")
SHAPE = (8, 2, 2, 4, 4)
VMEM_LIMIT = 16 * 1024 * 1024


def swap(value, axis, flip, size):
    return lax.ppermute(value, axis, [(i, i ^ flip) for i in range(size)])


def kernel_call(body, grid, ins, outs, out_shape, cost):
    return pl.pallas_call(
        body,
        grid=grid,
        in_specs=ins,
        out_specs=outs,
        out_shape=out_shape,
        compiler_params=pltpu.CompilerParams(vmem_limit_bytes=VMEM_LIMIT),
        cost_estimate=pl.CostEstimate(flops=cost, bytes_accessed=cost, transcendentals=0),
    )


SMEM = pl.BlockSpec(memory_space=pltpu.SMEM)


def place_of(block):
    row, col = block // 32, block % 32
    rows = pl.ds(pl.multiple_of(row * BLK, BLK), BLK)
    return rows, pl.ds(pl.multiple_of(col // 2 * LANES, LANES), LANES), col % 2


def lane_halves():
    return lax.broadcasted_iota(jnp.int32, (BLK, LANES), 1) // BLK


def product(at_ref, k, shards, cot_ref, left_ref, part_ref):
    for m, shard in enumerate(shards):

        @pl.when(at_ref[0] ^ k == m)
        def _(shard=shard):
            left_ref[...] = shard[...]

    for at in range(0, cot_ref.shape[1], 512):
        part_ref[:, at : at + 512] = lax.dot_general(
            left_ref[...],
            cot_ref[:, at : at + 512],
            (((0,), (0,)), ((), ())),
            preferred_element_type=F32,
        ).astype(BF16)


def pack(list_ref, k, base, count, part_ref, out_ref, lead=None):
    upper = lane_halves() == 1

    def tile(q, carry):
        sides = []
        for side in range(2):
            rows, cols, half = place_of(list_ref[k, base + 2 * q + side])
            block = part_ref[rows, cols]
            sides.append(jnp.where(half == side, block, pltpu.roll(block, BLK, 1)))
        at = pl.ds(pl.multiple_of(q * LANES, LANES), LANES)
        value = jnp.where(upper, sides[1], sides[0])
        if lead is None:
            out_ref[:, at] = value
        else:
            out_ref[lead, :, at] = value
        return carry

    lax.fori_loop(0, count // 2, tile, 0, unroll=True)


def first_kernel(row, list_ref, part_ref, out_ref):
    pack(list_ref, row, 0, HALF, part_ref, out_ref)


def rest_kernel(
    list_ref, at_ref, s0, s1, s2, s3, cot_ref,
    give_a, give_b, keep_a, keep_b, own_ref, left_ref, part_ref,
):
    shards, half = (s0, s1, s2, s3), HALF // 2
    low, high = 0, half
    product(at_ref, 1, shards, cot_ref, left_ref, part_ref)
    pack(list_ref, 1, low, half, part_ref, give_a, 0)
    pack(list_ref, 1, high, half, part_ref, keep_b)
    product(at_ref, 2, shards, cot_ref, left_ref, part_ref)
    pack(list_ref, 2, low, half, part_ref, give_a, 1)
    pack(list_ref, 2, high, half, part_ref, give_b, 1)
    product(at_ref, 3, shards, cot_ref, left_ref, part_ref)
    pack(list_ref, 3, high, half, part_ref, give_b, 0)
    pack(list_ref, 3, low, half, part_ref, keep_a)
    product(at_ref, 0, shards, cot_ref, left_ref, own_ref)


def products_call(body, lists, at, shards, cotangent, out_shape):
    whole = pl.BlockSpec(memory_space=pltpu.VMEM)
    depth, width = shards[0].shape
    cols = cotangent.shape[1]
    return pl.pallas_call(
        body,
        in_specs=[SMEM, SMEM] + [whole] * 5,
        out_specs=jax.tree.map(lambda _: whole, out_shape),
        out_shape=out_shape,
        scratch_shapes=[pltpu.VMEM((depth, width), BF16), pltpu.VMEM((width, cols), BF16)],
        compiler_params=pltpu.CompilerParams(vmem_limit_bytes=VMEM_LIMIT),
        cost_estimate=pl.CostEstimate(flops=1 << 20, bytes_accessed=1 << 20, transcendentals=0),
    )(lists, at, *shards, cotangent)


def packed(*lead, blocks=HALF):
    return jax.ShapeDtypeStruct((*lead, BLK, blocks * BLK), BF16)


def chosen_part(row, lists, part):
    whole = pl.BlockSpec(memory_space=pltpu.VMEM)
    body = functools.partial(first_kernel, row)
    return kernel_call(body, (), [SMEM, whole], whole, packed(), 1 << 20)(lists, part)


def rest_parts(lists, at, shards, cotangent):
    half = HALF // 2
    own = jax.ShapeDtypeStruct((shards[0].shape[1], cotangent.shape[1]), BF16)
    shapes = [packed(2, blocks=half)] * 2 + [packed(blocks=half)] * 2 + [own]
    return products_call(rest_kernel, lists, at, shards, cotangent, shapes)


def unpack(list_ref, base, count, terms, grad_ref):
    halves = lane_halves()

    def tile(q, carry):
        at = pl.ds(pl.multiple_of(q * LANES, LANES), LANES)
        value = terms[0](at).astype(F32)
        for term in terms[1:]:
            value = value + term(at).astype(F32)
        turned = pltpu.roll(value, BLK, 1)
        for side in range(2):
            rows, cols, half = place_of(list_ref[0, base + 2 * q + side])
            moved = jnp.where(half == side, value, turned)
            grad_ref[rows, cols] = jnp.where(halves == half, moved, grad_ref[rows, cols])
        return carry

    lax.fori_loop(0, count // 2, tile, 0, unroll=True)


def chosen_kernel(
    list_ref, c_ref, mask_ref, fb_ref, own_ref, got_1, got_2, got_3, mine_ref, other_ref, grad_ref
):
    row = pl.program_id(0)

    @pl.when(row == 0)
    def _():
        terms = [lambda at, ref=ref: ref[:, at] for ref in (got_1, got_2, got_3)]
        unpack(list_ref, 0, HALF, terms, grad_ref)

    first = c_ref[0] == 0
    rows = pl.ds(pl.multiple_of(row * BLK, BLK), BLK)
    for h in range(2):
        for yh in range(2):
            sent = []
            for c in range(2):
                at = h * 1024 + yh * 512 + c * 256
                at = slice(at, at + 256)
                acc = own_ref[:, at].astype(F32) + grad_ref[rows, at]
                acc = fb_ref[:, at].astype(F32) + acc
                chosen = jnp.broadcast_to(mask_ref[0, :, at], acc.shape) > 0.5
                sent.append(jnp.where(chosen, acc, 0.0))
            place = slice(yh * 256, yh * 256 + 256)
            mine_ref[h, :, place] = jnp.where(first, sent[0], sent[1])
            other_ref[h, :, place] = jnp.where(first, sent[1], sent[0]).astype(BF16)


def residual_kernel(
    list_ref, mask_ref, fb_ref, own_ref, got_a, got_b, next_a, next_b, new_ref, grad_ref
):
    row = pl.program_id(0)

    @pl.when(row == 0)
    def _():
        half = HALF // 2
        for base, got, nxt in ((0, got_a, next_a), (half, got_b, next_b)):
            terms = [lambda at, ref=got: ref[0, :, at], lambda at, ref=nxt: ref[:, at]]
            unpack(list_ref, base, half, terms, grad_ref)

    rows = pl.ds(pl.multiple_of(row * BLK, BLK), BLK)
    for at in range(0, fb_ref.shape[1], 256):
        at = slice(at, at + 256)
        acc = own_ref[:, at].astype(F32) + grad_ref[rows, at]
        acc = fb_ref[:, at].astype(F32) + acc
        chosen = jnp.broadcast_to(mask_ref[0, :, at], acc.shape) > 0.5
        new_ref[:, at] = jnp.where(chosen, 0.0, acc).astype(BF16)


def state_call(body, scalars, mask, feedback, own, received, outs, out_shape):
    rows, cols = feedback.shape
    wide = pl.BlockSpec((BLK, cols), lambda i: (i, 0))
    line = pl.BlockSpec((1, 1, cols), lambda i: (i, 0, 0))
    given = [pl.BlockSpec(r.shape, lambda i, n=r.ndim: (0,) * n) for r in received]
    return pl.pallas_call(
        body,
        grid=(rows // BLK,),
        in_specs=[SMEM] * len(scalars) + [line, wide, wide] + given,
        out_specs=outs,
        out_shape=out_shape,
        scratch_shapes=[pltpu.VMEM((rows, cols), F32)],
        compiler_params=pltpu.CompilerParams(vmem_limit_bytes=VMEM_LIMIT),
        cost_estimate=pl.CostEstimate(flops=1 << 22, bytes_accessed=1 << 22, transcendentals=0),
    )(*scalars, mask, feedback, own, *received)


def chosen_sums(lists, c, mask, feedback, own, *received):
    slab = pl.BlockSpec((2, BLK, 512), lambda i: (i, 0, 0))
    shape = (8, BLK, 512)
    return state_call(
        chosen_kernel, (lists, c), mask, feedback, own, received, [slab, slab],
        [jax.ShapeDtypeStruct(shape, F32), jax.ShapeDtypeStruct(shape, BF16)],
    )


def residual(lists, mask, feedback, own, *received):
    rows, cols = feedback.shape
    return state_call(
        residual_kernel, (lists,), mask, feedback, own, received,
        pl.BlockSpec((BLK, cols), lambda i: (i, 0)), jax.ShapeDtypeStruct((rows, cols), BF16),
    )


def owner_kernel(yh_ref, mine_ref, peer_ref, moment_ref, new_ref, step_ref):
    mean = (mine_ref[...] + peer_ref[...]) * (1.0 / NODES)
    moment = DECAY * moment_ref[...] + mean
    step = (mean + DECAY * moment).astype(BF16)
    for z in range(8):
        step_ref[z] = step
    own = jnp.where(yh_ref[0] == 0, moment[:, :256], moment[:, 256:])
    for b in range(4):
        new_ref[b] = own[:, b * BLK : (b + 1) * BLK]


def owner_update(yh, mine, peer, moment):
    whole = pl.BlockSpec(memory_space=pltpu.VMEM)
    return kernel_call(
        owner_kernel,
        (),
        [SMEM, whole, whole, whole],
        [whole, whole],
        [
            jax.ShapeDtypeStruct((4, BLK, BLK), F32),
            jax.ShapeDtypeStruct((8, BLK, 512), BF16),
        ],
        8 * BLK * 512,
    )(yh, mine, peer, moment)


def assemble_kernel(c_ref, mine_ref, other_ref, out_ref):
    first = c_ref[0] == 0
    for h in range(2):
        for yh in range(2):
            place = slice(yh * 256, yh * 256 + 256)
            mine, other = mine_ref[h, :, place], other_ref[h, :, place]
            at = h * 1024 + yh * 512
            out_ref[:, at : at + 256] = jnp.where(first, mine, other)
            out_ref[:, at + 256 : at + 512] = jnp.where(first, other, mine)


def assemble(c, mine, other, rows, cols):
    slab = pl.BlockSpec((2, BLK, 512), lambda i: (i, 0, 0))
    return kernel_call(
        assemble_kernel,
        (rows // BLK,),
        [SMEM, slab, slab],
        pl.BlockSpec((BLK, cols), lambda i: (i, 0)),
        jax.ShapeDtypeStruct((rows, cols), BF16),
        4 * rows * cols,
    )(c, mine, other)


def others_of(lists, count):
    blocks = jnp.arange(count, dtype=jnp.int32)
    left = jnp.all(lists[:, :, None] != blocks, axis=1)
    before = blocks[:, None] < blocks[None, :]
    rank = jnp.sum(jnp.where(left[:, :, None] & before, 1, 0), axis=1)
    slots = jnp.arange(count // 2, dtype=jnp.int32)
    hit = left[:, None, :] & (rank[:, None, :] == slots[None, :, None])
    return jnp.sum(jnp.where(hit, blocks, 0), axis=2)


def gather_hidden(hidden):
    far = swap(hidden, "t", 2, 4)
    near = swap(hidden, "t", 1, 4)
    return hidden, near, far, swap(far, "t", 1, 4)


def plus(kept, got):
    return (kept.astype(F32) + got.astype(F32)).astype(BF16)


def as_matrix(blocks):
    return blocks.transpose(1, 0, 2).reshape(BLK, -1)


def local(hidden, cotangent, feedback, chosen, momentum):
    rows, cols = feedback.shape[1:]
    rows_blk, cols_blk = rows // BLK, cols // BLK
    c, yh = lax.axis_index("c"), lax.axis_index("yh")
    at_c, at_yh = c.astype(jnp.int32).reshape(1), yh.astype(jnp.int32).reshape(1)
    block_of = (
        jnp.arange(rows_blk, dtype=jnp.int32)[:, None] * cols_blk
        + jnp.arange(cols, dtype=jnp.int32)[None, :] // BLK
    )
    mask = jnp.any(chosen.reshape(-1, 1, 1) == block_of[None], axis=0).astype(F32)
    moment = as_matrix(momentum[0, 0])
    mask = mask[:, None]
    picks = chosen.reshape(1, -1)
    near_picks = swap(picks, "dp", 1, 4)
    far_picks = swap(jnp.concatenate([picks, near_picks]), "dp", 3, 4)
    *shards, near_picks, far_picks = lax.optimization_barrier(
        (*gather_hidden(hidden), near_picks, far_picks)
    )
    at = (lax.axis_index("dp") ^ lax.axis_index("t")).astype(jnp.int32).reshape(1)
    got = {}
    for k, row, lists in ((2, 1, far_picks), (1, 0, near_picks), (3, 0, far_picks)):
        part = lax.dot_general(
            lax.select_n(at[0] ^ k, *shards),
            cotangent,
            (((0,), (0,)), ((), ())),
            preferred_element_type=F32,
        ).astype(BF16)
        given = chosen_part(row, lists, part)
        if k == 3:
            *shards, given, moment = lax.optimization_barrier((*shards, given, moment))
        else:
            *shards, _ = lax.optimization_barrier((*shards, given))
        got[k] = swap(given, "dp", k, 4)
    far_moment = swap(moment, "yh", 1, 2)
    others = jnp.concatenate([picks, near_picks, far_picks[1:], far_picks[:1]])
    others = others_of(others, rows_blk * cols_blk)
    rest = rest_parts(others, at, shards, cotangent)
    got_1, got_2, got_3, far_moment, give_a, give_b, keep_a, keep_b, own = (
        lax.optimization_barrier((got[1], got[2], got[3], far_moment, *rest))
    )
    mine, other = chosen_sums(picks, at_c, mask, feedback[0], own, got_1, got_2, got_3)
    pair = (mine + swap(other, "c", 1, 2).astype(F32)).astype(BF16)
    pair, give_a, give_b = lax.optimization_barrier((pair, give_a, give_b))
    got_a, got_b = swap(give_a, "dp", 1, 4), swap(give_b, "dp", 3, 4)
    across = lax.all_to_all(pair, "z", 0, 0, tiled=True)
    near = jnp.sum(across.astype(F32), axis=0)
    far = swap(near, "yh", 1, 2)
    far, got_a, got_b = lax.optimization_barrier((far, got_a, got_b))
    moment = jnp.where(
        yh == 0, jnp.concatenate([moment, far_moment], 1), jnp.concatenate([far_moment, moment], 1)
    )
    momentum_new, copies = owner_update(at_yh, near, far, moment)
    copies, got_a, got_b = lax.optimization_barrier((copies, got_a, got_b))
    next_a = swap(plus(keep_a, got_a[1]), "dp", 3, 4)
    next_b = swap(plus(keep_b, got_b[1]), "dp", 1, 4)
    every = lax.all_to_all(copies, "z", 0, 0, tiled=True)
    feedback_new = residual(others, mask, feedback[0], own, got_a, got_b, next_a, next_b)
    step = assemble(at_c, every, swap(every, "c", 1, 2), rows, cols)
    return feedback_new[None], momentum_new[None, None], step


def solution(mesh):
    fine = Mesh(mesh.devices.reshape(SHAPE), (*NODE, "dp", "t"))
    tokens = P((*NODE, "dp"), "t")
    return jax.shard_map(
        local,
        mesh=fine,
        in_specs=(
            tokens,
            tokens,
            P(NODE, "dp", "t"),
            P(NODE, "dp", "t", None),
            P("dp", "t", NODE, None, None),
        ),
        out_specs=(P(NODE, "dp", "t"), P("dp", "t", NODE, None, None), P("dp", "t")),
        check_vma=False,
    )
```

```python
import functools

import jax
import jax.numpy as jnp
from jax import lax
from jax.experimental import pallas as pl
from jax.experimental.pallas import tpu as pltpu
from jax.sharding import Mesh, PartitionSpec as P

BLK = 64
LANES = 128
HALF = 64
DECAY = 0.9
NODES = 32
F32, BF16 = jnp.float32, jnp.bfloat16
NODE = ("z", "yh", "c")
SHAPE = (8, 2, 2, 4, 4)
VMEM_LIMIT = 16 * 1024 * 1024


def swap(value, axis, flip, size):
    return lax.ppermute(value, axis, [(i, i ^ flip) for i in range(size)])


def kernel_call(body, grid, ins, outs, out_shape, cost):
    return pl.pallas_call(
        body,
        grid=grid,
        in_specs=ins,
        out_specs=outs,
        out_shape=out_shape,
        compiler_params=pltpu.CompilerParams(vmem_limit_bytes=VMEM_LIMIT),
        cost_estimate=pl.CostEstimate(flops=cost, bytes_accessed=cost, transcendentals=0),
    )


SMEM = pl.BlockSpec(memory_space=pltpu.SMEM)


def place_of(block):
    row, col = block // 32, block % 32
    rows = pl.ds(pl.multiple_of(row * BLK, BLK), BLK)
    return rows, pl.ds(pl.multiple_of(col // 2 * LANES, LANES), LANES), col % 2


def lane_halves():
    return lax.broadcasted_iota(jnp.int32, (BLK, LANES), 1) // BLK


def product(at_ref, k, shards, cot_ref, left_ref, part_ref):
    for m, shard in enumerate(shards):

        @pl.when(at_ref[0] ^ k == m)
        def _(shard=shard):
            left_ref[...] = shard[...]

    for at in range(0, cot_ref.shape[1], 512):
        part_ref[:, at : at + 512] = lax.dot_general(
            left_ref[...],
            cot_ref[:, at : at + 512],
            (((0,), (0,)), ((), ())),
            preferred_element_type=F32,
        ).astype(BF16)


def pack(list_ref, k, base, count, part_ref, out_ref, lead=None):
    upper = lane_halves() == 1

    def tile(q, carry):
        sides = []
        for side in range(2):
            rows, cols, half = place_of(list_ref[k, base + 2 * q + side])
            block = part_ref[rows, cols]
            sides.append(jnp.where(half == side, block, pltpu.roll(block, BLK, 1)))
        at = pl.ds(pl.multiple_of(q * LANES, LANES), LANES)
        value = jnp.where(upper, sides[1], sides[0])
        if lead is None:
            out_ref[:, at] = value
        else:
            out_ref[lead, :, at] = value
        return carry

    lax.fori_loop(0, count // 2, tile, 0, unroll=True)


def first_kernel(rows, *refs):
    n = len(rows)
    for row, list_ref, part_ref, out_ref in zip(rows, refs[:n], refs[n : 2 * n], refs[2 * n :]):
        pack(list_ref, row, 0, HALF, part_ref, out_ref)


def rest_kernel(
    list_ref, at_ref, s0, s1, s2, s3, cot_ref, give_ref, keep_ref, own_ref, left_ref, part_ref
):
    shards = (s0, s1, s2, s3)
    for lead, k in enumerate((1, 2)):
        product(at_ref, k, shards, cot_ref, left_ref, part_ref)
        pack(list_ref, k, 0, HALF, part_ref, give_ref, lead)
    product(at_ref, 3, shards, cot_ref, left_ref, part_ref)
    pack(list_ref, 3, 0, HALF, part_ref, keep_ref)
    product(at_ref, 0, shards, cot_ref, left_ref, own_ref)


def products_call(body, lists, at, shards, cotangent, out_shape):
    whole = pl.BlockSpec(memory_space=pltpu.VMEM)
    depth, width = shards[0].shape
    cols = cotangent.shape[1]
    return pl.pallas_call(
        body,
        in_specs=[SMEM, SMEM] + [whole] * 5,
        out_specs=jax.tree.map(lambda _: whole, out_shape),
        out_shape=out_shape,
        scratch_shapes=[pltpu.VMEM((depth, width), BF16), pltpu.VMEM((width, cols), BF16)],
        compiler_params=pltpu.CompilerParams(vmem_limit_bytes=VMEM_LIMIT),
        cost_estimate=pl.CostEstimate(flops=1 << 20, bytes_accessed=1 << 20, transcendentals=0),
    )(lists, at, *shards, cotangent)


def packed(*lead, blocks=HALF):
    return jax.ShapeDtypeStruct((*lead, BLK, blocks * BLK), BF16)


def chosen_parts(rows, lists, parts):
    whole, n = pl.BlockSpec(memory_space=pltpu.VMEM), len(rows)
    return kernel_call(
        functools.partial(first_kernel, rows),
        (),
        [SMEM] * n + [whole] * n,
        [whole] * n,
        [packed()] * n,
        1 << 20,
    )(*lists, *parts)


def rest_parts(lists, at, shards, cotangent):
    own = jax.ShapeDtypeStruct((shards[0].shape[1], cotangent.shape[1]), BF16)
    shapes = [packed(2), packed(), own]
    return products_call(rest_kernel, lists, at, shards, cotangent, shapes)


def unpack(list_ref, base, count, terms, grad_ref):
    halves = lane_halves()

    def tile(q, carry):
        at = pl.ds(pl.multiple_of(q * LANES, LANES), LANES)
        value = terms[0](at).astype(F32)
        for term in terms[1:]:
            value = value + term(at).astype(F32)
        turned = pltpu.roll(value, BLK, 1)
        for side in range(2):
            rows, cols, half = place_of(list_ref[0, base + 2 * q + side])
            moved = jnp.where(half == side, value, turned)
            grad_ref[rows, cols] = jnp.where(halves == half, moved, grad_ref[rows, cols])
        return carry

    lax.fori_loop(0, count // 2, tile, 0, unroll=True)


def chosen_kernel(
    list_ref, c_ref, mask_ref, fb_ref, own_ref, got_1, got_2, got_3, mine_ref, other_ref, grad_ref
):
    row = pl.program_id(0)

    @pl.when(row == 0)
    def _():
        terms = [lambda at, ref=ref: ref[:, at] for ref in (got_1, got_2, got_3)]
        unpack(list_ref, 0, HALF, terms, grad_ref)

    first = c_ref[0] == 0
    rows = pl.ds(pl.multiple_of(row * BLK, BLK), BLK)
    for h in range(2):
        for yh in range(2):
            sent = []
            for c in range(2):
                at = h * 1024 + yh * 512 + c * 256
                at = slice(at, at + 256)
                acc = own_ref[:, at].astype(F32) + grad_ref[rows, at]
                acc = fb_ref[:, at].astype(F32) + acc
                chosen = jnp.broadcast_to(mask_ref[0, :, at], acc.shape) > 0.5
                sent.append(jnp.where(chosen, acc, 0.0))
            place = slice(yh * 256, yh * 256 + 256)
            mine_ref[h, :, place] = jnp.where(first, sent[0], sent[1])
            other_ref[h, :, place] = jnp.where(first, sent[1], sent[0]).astype(BF16)


def residual_kernel(list_ref, mask_ref, fb_ref, own_ref, got, nxt, new_ref, grad_ref):
    row = pl.program_id(0)

    @pl.when(row == 0)
    def _():
        terms = [lambda at: got[0, :, at], lambda at: nxt[:, at]]
        unpack(list_ref, 0, HALF, terms, grad_ref)

    rows = pl.ds(pl.multiple_of(row * BLK, BLK), BLK)
    for at in range(0, fb_ref.shape[1], 256):
        at = slice(at, at + 256)
        acc = own_ref[:, at].astype(F32) + grad_ref[rows, at]
        acc = fb_ref[:, at].astype(F32) + acc
        chosen = jnp.broadcast_to(mask_ref[0, :, at], acc.shape) > 0.5
        new_ref[:, at] = jnp.where(chosen, 0.0, acc).astype(BF16)


def state_call(body, scalars, mask, feedback, own, received, outs, out_shape):
    rows, cols = feedback.shape
    wide = pl.BlockSpec((BLK, cols), lambda i: (i, 0))
    line = pl.BlockSpec((1, 1, cols), lambda i: (i, 0, 0))
    given = [pl.BlockSpec(r.shape, lambda i, n=r.ndim: (0,) * n) for r in received]
    return pl.pallas_call(
        body,
        grid=(rows // BLK,),
        in_specs=[SMEM] * len(scalars) + [line, wide, wide] + given,
        out_specs=outs,
        out_shape=out_shape,
        scratch_shapes=[pltpu.VMEM((rows, cols), F32)],
        compiler_params=pltpu.CompilerParams(vmem_limit_bytes=VMEM_LIMIT),
        cost_estimate=pl.CostEstimate(flops=1 << 22, bytes_accessed=1 << 22, transcendentals=0),
    )(*scalars, mask, feedback, own, *received)


def chosen_sums(lists, c, mask, feedback, own, *received):
    slab = pl.BlockSpec((2, BLK, 512), lambda i: (i, 0, 0))
    shape = (8, BLK, 512)
    return state_call(
        chosen_kernel, (lists, c), mask, feedback, own, received, [slab, slab],
        [jax.ShapeDtypeStruct(shape, F32), jax.ShapeDtypeStruct(shape, BF16)],
    )


def residual(lists, mask, feedback, own, *received):
    rows, cols = feedback.shape
    return state_call(
        residual_kernel, (lists,), mask, feedback, own, received,
        pl.BlockSpec((BLK, cols), lambda i: (i, 0)), jax.ShapeDtypeStruct((rows, cols), BF16),
    )


def owner_kernel(yh_ref, mine_ref, peer_ref, moment_ref, new_ref, step_ref):
    mean = (mine_ref[...] + peer_ref[...]) * (1.0 / NODES)
    moment = DECAY * moment_ref[...] + mean
    step = (mean + DECAY * moment).astype(BF16)
    for z in range(8):
        step_ref[z] = step
    own = jnp.where(yh_ref[0] == 0, moment[:, :256], moment[:, 256:])
    for b in range(4):
        new_ref[b] = own[:, b * BLK : (b + 1) * BLK]


def owner_update(yh, mine, peer, moment):
    whole = pl.BlockSpec(memory_space=pltpu.VMEM)
    return kernel_call(
        owner_kernel,
        (),
        [SMEM, whole, whole, whole],
        [whole, whole],
        [
            jax.ShapeDtypeStruct((4, BLK, BLK), F32),
            jax.ShapeDtypeStruct((8, BLK, 512), BF16),
        ],
        8 * BLK * 512,
    )(yh, mine, peer, moment)


def assemble_kernel(c_ref, mine_ref, other_ref, out_ref):
    first = c_ref[0] == 0
    for h in range(2):
        for yh in range(2):
            place = slice(yh * 256, yh * 256 + 256)
            mine, other = mine_ref[h, :, place], other_ref[h, :, place]
            at = h * 1024 + yh * 512
            out_ref[:, at : at + 256] = jnp.where(first, mine, other)
            out_ref[:, at + 256 : at + 512] = jnp.where(first, other, mine)


def assemble(c, mine, other, rows, cols):
    slab = pl.BlockSpec((2, BLK, 512), lambda i: (i, 0, 0))
    return kernel_call(
        assemble_kernel,
        (rows // BLK,),
        [SMEM, slab, slab],
        pl.BlockSpec((BLK, cols), lambda i: (i, 0)),
        jax.ShapeDtypeStruct((rows, cols), BF16),
        4 * rows * cols,
    )(c, mine, other)


def others_of(lists, count):
    blocks = jnp.arange(count, dtype=jnp.int32)
    left = jnp.all(lists[:, :, None] != blocks, axis=1)
    before = blocks[:, None] < blocks[None, :]
    rank = jnp.sum(jnp.where(left[:, :, None] & before, 1, 0), axis=1)
    slots = jnp.arange(count // 2, dtype=jnp.int32)
    hit = left[:, None, :] & (rank[:, None, :] == slots[None, :, None])
    return jnp.sum(jnp.where(hit, blocks, 0), axis=2)


def gather_hidden(hidden):
    far = swap(hidden, "t", 2, 4)
    near = swap(hidden, "t", 1, 4)
    return hidden, near, far, swap(far, "t", 1, 4)


def plus(kept, got):
    return (kept.astype(F32) + got.astype(F32)).astype(BF16)


def as_matrix(blocks):
    return blocks.transpose(1, 0, 2).reshape(BLK, -1)


def local(hidden, cotangent, feedback, chosen, momentum):
    rows, cols = feedback.shape[1:]
    rows_blk, cols_blk = rows // BLK, cols // BLK
    c, yh = lax.axis_index("c"), lax.axis_index("yh")
    at_c, at_yh = c.astype(jnp.int32).reshape(1), yh.astype(jnp.int32).reshape(1)
    block_of = (
        jnp.arange(rows_blk, dtype=jnp.int32)[:, None] * cols_blk
        + jnp.arange(cols, dtype=jnp.int32)[None, :] // BLK
    )
    mask = jnp.any(chosen.reshape(-1, 1, 1) == block_of[None], axis=0).astype(F32)
    moment = as_matrix(momentum[0, 0])
    mask = mask[:, None]
    picks = chosen.reshape(1, -1)
    near_picks = swap(picks, "dp", 1, 4)
    far_picks = swap(jnp.concatenate([picks, near_picks]), "dp", 3, 4)
    *shards, near_picks, far_picks = lax.optimization_barrier(
        (*gather_hidden(hidden), near_picks, far_picks)
    )
    at = (lax.axis_index("dp") ^ lax.axis_index("t")).astype(jnp.int32).reshape(1)

    def part(k, shards):
        return lax.dot_general(
            lax.select_n(at[0] ^ k, *shards),
            cotangent,
            (((0,), (0,)), ((), ())),
            preferred_element_type=F32,
        ).astype(BF16)

    (give_2,) = chosen_parts((1,), (far_picks,), (part(2, shards),))
    got_2 = swap(give_2, "dp", 2, 4)
    *shards, _ = lax.optimization_barrier((*shards, give_2))
    give_1, give_3 = chosen_parts(
        (0, 0), (near_picks, far_picks), (part(1, shards), part(3, shards))
    )
    got_1 = swap(give_1, "dp", 1, 4)
    *shards, give_3, moment = lax.optimization_barrier((*shards, give_3, moment))
    got_3 = swap(give_3, "dp", 3, 4)
    far_moment = swap(moment, "yh", 1, 2)
    others = jnp.concatenate([picks, near_picks, far_picks[1:], far_picks[:1]])
    others = others_of(others, rows_blk * cols_blk)
    rest = rest_parts(others, at, shards, cotangent)
    got_1, got_2, got_3, far_moment, give, keep, own = lax.optimization_barrier(
        (got_1, got_2, got_3, far_moment, *rest)
    )
    mine, other = chosen_sums(picks, at_c, mask, feedback[0], own, got_1, got_2, got_3)
    pair = (mine + swap(other, "c", 1, 2).astype(F32)).astype(BF16)
    pair, give = lax.optimization_barrier((pair, give))
    got_rest = swap(give, "dp", 1, 4)
    across = lax.all_to_all(pair, "z", 0, 0, tiled=True)
    near = jnp.sum(across.astype(F32), axis=0)
    far = swap(near, "yh", 1, 2)
    far, give_rest = lax.optimization_barrier((far, plus(keep, got_rest[1])))
    moment = jnp.where(
        yh == 0, jnp.concatenate([moment, far_moment], 1), jnp.concatenate([far_moment, moment], 1)
    )
    momentum_new, copies = owner_update(at_yh, near, far, moment)
    next_rest = swap(give_rest, "dp", 3, 4)
    every = lax.all_to_all(copies, "z", 0, 0, tiled=True)
    feedback_new = residual(others, mask, feedback[0], own, got_rest, next_rest)
    step = assemble(at_c, every, swap(every, "c", 1, 2), rows, cols)
    return feedback_new[None], momentum_new[None, None], step


def solution(mesh):
    fine = Mesh(mesh.devices.reshape(SHAPE), (*NODE, "dp", "t"))
    tokens = P((*NODE, "dp"), "t")
    return jax.shard_map(
        local,
        mesh=fine,
        in_specs=(
            tokens,
            tokens,
            P(NODE, "dp", "t"),
            P(NODE, "dp", "t", None),
            P("dp", "t", NODE, None, None),
        ),
        out_specs=(P(NODE, "dp", "t"), P("dp", "t", NODE, None, None), P("dp", "t")),
        check_vma=False,
    )
```

```python
import functools

import jax
import jax.numpy as jnp
from jax import lax
from jax.experimental import pallas as pl
from jax.experimental.pallas import tpu as pltpu
from jax.sharding import Mesh, PartitionSpec as P

BLK = 64
LANES = 128
HALF = 64
DECAY = 0.9
NODES = 32
F32, BF16 = jnp.float32, jnp.bfloat16
NODE = ("z", "yh", "c")
SHAPE = (8, 2, 2, 4, 4)
VMEM_LIMIT = 16 * 1024 * 1024


def swap(value, axis, flip, size):
    return lax.ppermute(value, axis, [(i, i ^ flip) for i in range(size)])


def kernel_call(body, grid, ins, outs, out_shape, cost):
    return pl.pallas_call(
        body,
        grid=grid,
        in_specs=ins,
        out_specs=outs,
        out_shape=out_shape,
        compiler_params=pltpu.CompilerParams(vmem_limit_bytes=VMEM_LIMIT),
        cost_estimate=pl.CostEstimate(flops=cost, bytes_accessed=cost, transcendentals=0),
    )


SMEM = pl.BlockSpec(memory_space=pltpu.SMEM)


def place_of(block):
    row, col = block // 32, block % 32
    rows = pl.ds(pl.multiple_of(row * BLK, BLK), BLK)
    return rows, pl.ds(pl.multiple_of(col // 2 * LANES, LANES), LANES), col % 2


def lane_halves():
    return lax.broadcasted_iota(jnp.int32, (BLK, LANES), 1) // BLK


def product(at_ref, k, shards, cot_ref, left_ref, part_ref):
    for m, shard in enumerate(shards):

        @pl.when(at_ref[0] ^ k == m)
        def _(shard=shard):
            left_ref[...] = shard[...]

    for at in range(0, cot_ref.shape[1], 512):
        part_ref[:, at : at + 512] = lax.dot_general(
            left_ref[...],
            cot_ref[:, at : at + 512],
            (((0,), (0,)), ((), ())),
            preferred_element_type=F32,
        ).astype(BF16)


def pack(list_ref, k, base, count, part_ref, out_ref, lead=None):
    upper = lane_halves() == 1

    def tile(q, carry):
        sides = []
        for side in range(2):
            rows, cols, half = place_of(list_ref[k, base + 2 * q + side])
            block = part_ref[rows, cols]
            sides.append(jnp.where(half == side, block, pltpu.roll(block, BLK, 1)))
        at = pl.ds(pl.multiple_of(q * LANES, LANES), LANES)
        value = jnp.where(upper, sides[1], sides[0])
        if lead is None:
            out_ref[:, at] = value
        else:
            out_ref[lead, :, at] = value
        return carry

    lax.fori_loop(0, count // 2, tile, 0, unroll=True)


def first_kernel(rows, *refs):
    n = len(rows)
    for row, list_ref, part_ref, out_ref in zip(rows, refs[:n], refs[n : 2 * n], refs[2 * n :]):
        pack(list_ref, row, 0, HALF, part_ref, out_ref)


def rest_kernel(
    list_ref, at_ref, s0, s1, s2, s3, cot_ref,
    give_a, give_b, keep_a, keep_b, own_ref, left_ref, part_ref,
):
    shards, half = (s0, s1, s2, s3), HALF // 2
    product(at_ref, 1, shards, cot_ref, left_ref, part_ref)
    pack(list_ref, 1, 0, half, part_ref, give_a, 0)
    pack(list_ref, 1, half, half, part_ref, keep_b)
    product(at_ref, 2, shards, cot_ref, left_ref, part_ref)
    pack(list_ref, 2, 0, half, part_ref, give_a, 1)
    pack(list_ref, 2, half, half, part_ref, give_b, 1)
    product(at_ref, 3, shards, cot_ref, left_ref, part_ref)
    pack(list_ref, 3, half, half, part_ref, give_b, 0)
    pack(list_ref, 3, 0, half, part_ref, keep_a)
    product(at_ref, 0, shards, cot_ref, left_ref, own_ref)


def products_call(body, lists, at, shards, cotangent, out_shape):
    whole = pl.BlockSpec(memory_space=pltpu.VMEM)
    depth, width = shards[0].shape
    cols = cotangent.shape[1]
    return pl.pallas_call(
        body,
        in_specs=[SMEM, SMEM] + [whole] * 5,
        out_specs=jax.tree.map(lambda _: whole, out_shape),
        out_shape=out_shape,
        scratch_shapes=[pltpu.VMEM((depth, width), BF16), pltpu.VMEM((width, cols), BF16)],
        compiler_params=pltpu.CompilerParams(vmem_limit_bytes=VMEM_LIMIT),
        cost_estimate=pl.CostEstimate(flops=1 << 20, bytes_accessed=1 << 20, transcendentals=0),
    )(lists, at, *shards, cotangent)


def packed(*lead, blocks=HALF):
    return jax.ShapeDtypeStruct((*lead, BLK, blocks * BLK), BF16)


def chosen_parts(rows, lists, parts):
    whole, n = pl.BlockSpec(memory_space=pltpu.VMEM), len(rows)
    return kernel_call(
        functools.partial(first_kernel, rows),
        (),
        [SMEM] * n + [whole] * n,
        [whole] * n,
        [packed()] * n,
        1 << 20,
    )(*lists, *parts)


def rest_parts(lists, at, shards, cotangent):
    own = jax.ShapeDtypeStruct((shards[0].shape[1], cotangent.shape[1]), BF16)
    half = HALF // 2
    shapes = [packed(2, blocks=half)] * 2 + [packed(blocks=half)] * 2 + [own]
    return products_call(rest_kernel, lists, at, shards, cotangent, shapes)


def unpack(list_ref, base, count, terms, grad_ref):
    halves = lane_halves()

    def tile(q, carry):
        at = pl.ds(pl.multiple_of(q * LANES, LANES), LANES)
        value = terms[0](at).astype(F32)
        for term in terms[1:]:
            value = value + term(at).astype(F32)
        turned = pltpu.roll(value, BLK, 1)
        for side in range(2):
            rows, cols, half = place_of(list_ref[0, base + 2 * q + side])
            moved = jnp.where(half == side, value, turned)
            grad_ref[rows, cols] = jnp.where(halves == half, moved, grad_ref[rows, cols])
        return carry

    lax.fori_loop(0, count // 2, tile, 0, unroll=True)


def chosen_kernel(
    list_ref, c_ref, mask_ref, fb_ref, own_ref, got_1, got_2, got_3, mine_ref, other_ref, grad_ref
):
    row = pl.program_id(0)

    @pl.when(row == 0)
    def _():
        terms = [lambda at, ref=ref: ref[:, at] for ref in (got_1, got_2, got_3)]
        unpack(list_ref, 0, HALF, terms, grad_ref)

    first = c_ref[0] == 0
    rows = pl.ds(pl.multiple_of(row * BLK, BLK), BLK)
    for h in range(2):
        for yh in range(2):
            sent = []
            for c in range(2):
                at = h * 1024 + yh * 512 + c * 256
                at = slice(at, at + 256)
                acc = own_ref[:, at].astype(F32) + grad_ref[rows, at]
                acc = fb_ref[:, at].astype(F32) + acc
                chosen = jnp.broadcast_to(mask_ref[0, :, at], acc.shape) > 0.5
                sent.append(jnp.where(chosen, acc, 0.0))
            place = slice(yh * 256, yh * 256 + 256)
            mine_ref[h, :, place] = jnp.where(first, sent[0], sent[1])
            other_ref[h, :, place] = jnp.where(first, sent[1], sent[0]).astype(BF16)


def residual_kernel(
    list_ref, mask_ref, fb_ref, own_ref, got_a, got_b, next_a, next_b, new_ref, grad_ref
):
    row = pl.program_id(0)

    @pl.when(row == 0)
    def _():
        half = HALF // 2
        for base, got, nxt in ((0, got_a, next_a), (half, got_b, next_b)):
            terms = [lambda at, ref=got: ref[0, :, at], lambda at, ref=nxt: ref[:, at]]
            unpack(list_ref, base, half, terms, grad_ref)

    rows = pl.ds(pl.multiple_of(row * BLK, BLK), BLK)
    for at in range(0, fb_ref.shape[1], 256):
        at = slice(at, at + 256)
        acc = own_ref[:, at].astype(F32) + grad_ref[rows, at]
        acc = fb_ref[:, at].astype(F32) + acc
        chosen = jnp.broadcast_to(mask_ref[0, :, at], acc.shape) > 0.5
        new_ref[:, at] = jnp.where(chosen, 0.0, acc).astype(BF16)


def state_call(body, scalars, mask, feedback, own, received, outs, out_shape):
    rows, cols = feedback.shape
    wide = pl.BlockSpec((BLK, cols), lambda i: (i, 0))
    line = pl.BlockSpec((1, 1, cols), lambda i: (i, 0, 0))
    given = [pl.BlockSpec(r.shape, lambda i, n=r.ndim: (0,) * n) for r in received]
    return pl.pallas_call(
        body,
        grid=(rows // BLK,),
        in_specs=[SMEM] * len(scalars) + [line, wide, wide] + given,
        out_specs=outs,
        out_shape=out_shape,
        scratch_shapes=[pltpu.VMEM((rows, cols), F32)],
        compiler_params=pltpu.CompilerParams(vmem_limit_bytes=VMEM_LIMIT),
        cost_estimate=pl.CostEstimate(flops=1 << 22, bytes_accessed=1 << 22, transcendentals=0),
    )(*scalars, mask, feedback, own, *received)


def chosen_sums(lists, c, mask, feedback, own, *received):
    slab = pl.BlockSpec((2, BLK, 512), lambda i: (i, 0, 0))
    shape = (8, BLK, 512)
    return state_call(
        chosen_kernel, (lists, c), mask, feedback, own, received, [slab, slab],
        [jax.ShapeDtypeStruct(shape, F32), jax.ShapeDtypeStruct(shape, BF16)],
    )


def residual(lists, mask, feedback, own, *received):
    rows, cols = feedback.shape
    return state_call(
        residual_kernel, (lists,), mask, feedback, own, received,
        pl.BlockSpec((BLK, cols), lambda i: (i, 0)), jax.ShapeDtypeStruct((rows, cols), BF16),
    )


def owner_kernel(yh_ref, mine_ref, peer_ref, moment_ref, new_ref, step_ref):
    mean = (mine_ref[...] + peer_ref[...]) * (1.0 / NODES)
    moment = DECAY * moment_ref[...] + mean
    step = (mean + DECAY * moment).astype(BF16)
    for z in range(8):
        step_ref[z] = step
    own = jnp.where(yh_ref[0] == 0, moment[:, :256], moment[:, 256:])
    for b in range(4):
        new_ref[b] = own[:, b * BLK : (b + 1) * BLK]


def owner_update(yh, mine, peer, moment):
    whole = pl.BlockSpec(memory_space=pltpu.VMEM)
    return kernel_call(
        owner_kernel,
        (),
        [SMEM, whole, whole, whole],
        [whole, whole],
        [
            jax.ShapeDtypeStruct((4, BLK, BLK), F32),
            jax.ShapeDtypeStruct((8, BLK, 512), BF16),
        ],
        8 * BLK * 512,
    )(yh, mine, peer, moment)


def assemble_kernel(c_ref, mine_ref, other_ref, out_ref):
    first = c_ref[0] == 0
    for h in range(2):
        for yh in range(2):
            place = slice(yh * 256, yh * 256 + 256)
            mine, other = mine_ref[h, :, place], other_ref[h, :, place]
            at = h * 1024 + yh * 512
            out_ref[:, at : at + 256] = jnp.where(first, mine, other)
            out_ref[:, at + 256 : at + 512] = jnp.where(first, other, mine)


def assemble(c, mine, other, rows, cols):
    slab = pl.BlockSpec((2, BLK, 512), lambda i: (i, 0, 0))
    return kernel_call(
        assemble_kernel,
        (rows // BLK,),
        [SMEM, slab, slab],
        pl.BlockSpec((BLK, cols), lambda i: (i, 0)),
        jax.ShapeDtypeStruct((rows, cols), BF16),
        4 * rows * cols,
    )(c, mine, other)


def others_of(lists, count):
    blocks = jnp.arange(count, dtype=jnp.int32)
    left = jnp.all(lists[:, :, None] != blocks, axis=1)
    before = blocks[:, None] < blocks[None, :]
    rank = jnp.sum(jnp.where(left[:, :, None] & before, 1, 0), axis=1)
    slots = jnp.arange(count // 2, dtype=jnp.int32)
    hit = left[:, None, :] & (rank[:, None, :] == slots[None, :, None])
    return jnp.sum(jnp.where(hit, blocks, 0), axis=2)


def gather_hidden(hidden):
    far = swap(hidden, "t", 2, 4)
    near = swap(hidden, "t", 1, 4)
    return hidden, near, far, swap(far, "t", 1, 4)


def plus(kept, got):
    return (kept.astype(F32) + got.astype(F32)).astype(BF16)


def as_matrix(blocks):
    return blocks.transpose(1, 0, 2).reshape(BLK, -1)


def local(hidden, cotangent, feedback, chosen, momentum):
    rows, cols = feedback.shape[1:]
    rows_blk, cols_blk = rows // BLK, cols // BLK
    c, yh = lax.axis_index("c"), lax.axis_index("yh")
    at_c, at_yh = c.astype(jnp.int32).reshape(1), yh.astype(jnp.int32).reshape(1)
    block_of = (
        jnp.arange(rows_blk, dtype=jnp.int32)[:, None] * cols_blk
        + jnp.arange(cols, dtype=jnp.int32)[None, :] // BLK
    )
    mask = jnp.any(chosen.reshape(-1, 1, 1) == block_of[None], axis=0).astype(F32)
    moment = as_matrix(momentum[0, 0])
    mask = mask[:, None]
    picks = chosen.reshape(1, -1)
    near_picks = swap(picks, "dp", 1, 4)
    far_picks = swap(jnp.concatenate([picks, near_picks]), "dp", 3, 4)
    *shards, near_picks, far_picks = lax.optimization_barrier(
        (*gather_hidden(hidden), near_picks, far_picks)
    )
    at = (lax.axis_index("dp") ^ lax.axis_index("t")).astype(jnp.int32).reshape(1)

    def part(k, shards):
        return lax.dot_general(
            lax.select_n(at[0] ^ k, *shards),
            cotangent,
            (((0,), (0,)), ((), ())),
            preferred_element_type=F32,
        ).astype(BF16)

    (give_2,) = chosen_parts((1,), (far_picks,), (part(2, shards),))
    got_2 = swap(give_2, "dp", 2, 4)
    *shards, _ = lax.optimization_barrier((*shards, give_2))
    give_1, give_3 = chosen_parts(
        (0, 0), (near_picks, far_picks), (part(1, shards), part(3, shards))
    )
    got_1 = swap(give_1, "dp", 1, 4)
    *shards, give_3, moment = lax.optimization_barrier((*shards, give_3, moment))
    got_3 = swap(give_3, "dp", 3, 4)
    far_moment = swap(moment, "yh", 1, 2)
    others = jnp.concatenate([picks, near_picks, far_picks[1:], far_picks[:1]])
    others = others_of(others, rows_blk * cols_blk)
    rest = rest_parts(others, at, shards, cotangent)
    got_1, got_2, got_3, far_moment, give_a, give_b, keep_a, keep_b, own = (
        lax.optimization_barrier((got_1, got_2, got_3, far_moment, *rest))
    )
    mine, other = chosen_sums(picks, at_c, mask, feedback[0], own, got_1, got_2, got_3)
    pair = (mine + swap(other, "c", 1, 2).astype(F32)).astype(BF16)
    pair, give_a, give_b = lax.optimization_barrier((pair, give_a, give_b))
    got_a, got_b = swap(give_a, "dp", 1, 4), swap(give_b, "dp", 3, 4)
    across = lax.all_to_all(pair, "z", 0, 0, tiled=True)
    near = jnp.sum(across.astype(F32), axis=0)
    near, keep_a, keep_b = lax.optimization_barrier((near, keep_a, keep_b))
    far = swap(near, "yh", 1, 2)
    far, give_a, give_b = lax.optimization_barrier(
        (far, plus(keep_a, got_a[1]), plus(keep_b, got_b[1]))
    )
    moment = jnp.where(
        yh == 0, jnp.concatenate([moment, far_moment], 1), jnp.concatenate([far_moment, moment], 1)
    )
    momentum_new, copies = owner_update(at_yh, near, far, moment)
    next_a, next_b = swap(give_a, "dp", 3, 4), swap(give_b, "dp", 1, 4)
    every = lax.all_to_all(copies, "z", 0, 0, tiled=True)
    every, next_a, next_b = lax.optimization_barrier((every, next_a, next_b))
    feedback_new = residual(others, mask, feedback[0], own, got_a, got_b, next_a, next_b)
    step = assemble(at_c, every, swap(every, "c", 1, 2), rows, cols)
    return feedback_new[None], momentum_new[None, None], step


def solution(mesh):
    fine = Mesh(mesh.devices.reshape(SHAPE), (*NODE, "dp", "t"))
    tokens = P((*NODE, "dp"), "t")
    return jax.shard_map(
        local,
        mesh=fine,
        in_specs=(
            tokens,
            tokens,
            P(NODE, "dp", "t"),
            P(NODE, "dp", "t", None),
            P("dp", "t", NODE, None, None),
        ),
        out_specs=(P(NODE, "dp", "t"), P("dp", "t", NODE, None, None), P("dp", "t")),
        check_vma=False,
    )
```

```python
import functools

import jax
import jax.numpy as jnp
from jax import lax
from jax.experimental import pallas as pl
from jax.experimental.pallas import tpu as pltpu
from jax.sharding import Mesh, PartitionSpec as P

BLK = 64
LANES = 128
HALF = 64
DECAY = 0.9
NODES = 32
F32, BF16 = jnp.float32, jnp.bfloat16
NODE = ("z", "yh", "c")
SHAPE = (8, 2, 2, 4, 4)
VMEM_LIMIT = 16 * 1024 * 1024


def swap(value, axis, flip, size):
    return lax.ppermute(value, axis, [(i, i ^ flip) for i in range(size)])


def kernel_call(body, grid, ins, outs, out_shape, cost):
    return pl.pallas_call(
        body,
        grid=grid,
        in_specs=ins,
        out_specs=outs,
        out_shape=out_shape,
        compiler_params=pltpu.CompilerParams(vmem_limit_bytes=VMEM_LIMIT),
        cost_estimate=pl.CostEstimate(flops=cost, bytes_accessed=cost, transcendentals=0),
    )


SMEM = pl.BlockSpec(memory_space=pltpu.SMEM)


def place_of(block):
    row, col = block // 32, block % 32
    rows = pl.ds(pl.multiple_of(row * BLK, BLK), BLK)
    return rows, pl.ds(pl.multiple_of(col // 2 * LANES, LANES), LANES), col % 2


def lane_halves():
    return lax.broadcasted_iota(jnp.int32, (BLK, LANES), 1) // BLK


def product(at_ref, k, shards, cot_ref, left_ref, part_ref):
    for m, shard in enumerate(shards):

        @pl.when(at_ref[0] ^ k == m)
        def _(shard=shard):
            left_ref[...] = shard[...]

    for at in range(0, cot_ref.shape[1], 512):
        part_ref[:, at : at + 512] = lax.dot_general(
            left_ref[...],
            cot_ref[:, at : at + 512],
            (((0,), (0,)), ((), ())),
            preferred_element_type=F32,
        ).astype(BF16)


def pack(list_ref, k, base, count, part_ref, out_ref, lead=None):
    upper = lane_halves() == 1

    def tile(q, carry):
        sides = []
        for side in range(2):
            rows, cols, half = place_of(list_ref[k, base + 2 * q + side])
            block = part_ref[rows, cols]
            sides.append(jnp.where(half == side, block, pltpu.roll(block, BLK, 1)))
        at = pl.ds(pl.multiple_of(q * LANES, LANES), LANES)
        value = jnp.where(upper, sides[1], sides[0])
        if lead is None:
            out_ref[:, at] = value
        else:
            out_ref[lead, :, at] = value
        return carry

    lax.fori_loop(0, count // 2, tile, 0, unroll=True)


def first_kernel(rows, *refs):
    n = len(rows)
    for row, list_ref, part_ref, out_ref in zip(rows, refs[:n], refs[n : 2 * n], refs[2 * n :]):
        pack(list_ref, row, 0, HALF, part_ref, out_ref)


def rest_kernel(
    list_ref, at_ref, s0, s1, s2, s3, cot_ref, give_ref, keep_ref, own_ref, left_ref, part_ref
):
    shards = (s0, s1, s2, s3)
    for lead, k in enumerate((1, 2)):
        product(at_ref, k, shards, cot_ref, left_ref, part_ref)
        pack(list_ref, k, 0, HALF, part_ref, give_ref, lead)
    product(at_ref, 3, shards, cot_ref, left_ref, part_ref)
    pack(list_ref, 3, 0, HALF, part_ref, keep_ref)
    product(at_ref, 0, shards, cot_ref, left_ref, own_ref)


def products_call(body, lists, at, shards, cotangent, out_shape):
    whole = pl.BlockSpec(memory_space=pltpu.VMEM)
    depth, width = shards[0].shape
    cols = cotangent.shape[1]
    return pl.pallas_call(
        body,
        in_specs=[SMEM, SMEM] + [whole] * 5,
        out_specs=jax.tree.map(lambda _: whole, out_shape),
        out_shape=out_shape,
        scratch_shapes=[pltpu.VMEM((depth, width), BF16), pltpu.VMEM((width, cols), BF16)],
        compiler_params=pltpu.CompilerParams(vmem_limit_bytes=VMEM_LIMIT),
        cost_estimate=pl.CostEstimate(flops=1 << 20, bytes_accessed=1 << 20, transcendentals=0),
    )(lists, at, *shards, cotangent)


def packed(*lead, blocks=HALF):
    return jax.ShapeDtypeStruct((*lead, BLK, blocks * BLK), BF16)


def chosen_parts(rows, lists, parts):
    whole, n = pl.BlockSpec(memory_space=pltpu.VMEM), len(rows)
    return kernel_call(
        functools.partial(first_kernel, rows),
        (),
        [SMEM] * n + [whole] * n,
        [whole] * n,
        [packed()] * n,
        1 << 20,
    )(*lists, *parts)


def rest_parts(lists, at, shards, cotangent):
    own = jax.ShapeDtypeStruct((shards[0].shape[1], cotangent.shape[1]), BF16)
    shapes = [packed(2), packed(), own]
    return products_call(rest_kernel, lists, at, shards, cotangent, shapes)


def unpack(list_ref, base, count, terms, grad_ref):
    halves = lane_halves()

    def tile(q, carry):
        at = pl.ds(pl.multiple_of(q * LANES, LANES), LANES)
        value = terms[0](at).astype(F32)
        for term in terms[1:]:
            value = value + term(at).astype(F32)
        turned = pltpu.roll(value, BLK, 1)
        for side in range(2):
            rows, cols, half = place_of(list_ref[0, base + 2 * q + side])
            moved = jnp.where(half == side, value, turned)
            grad_ref[rows, cols] = jnp.where(halves == half, moved, grad_ref[rows, cols])
        return carry

    lax.fori_loop(0, count // 2, tile, 0, unroll=True)


def chosen_kernel(
    list_ref, c_ref, mask_ref, fb_ref, own_ref, got_1, got_2, got_3, mine_ref, other_ref, grad_ref
):
    row = pl.program_id(0)

    @pl.when(row == 0)
    def _():
        terms = [lambda at, ref=ref: ref[:, at] for ref in (got_1, got_2, got_3)]
        unpack(list_ref, 0, HALF, terms, grad_ref)

    first = c_ref[0] == 0
    rows = pl.ds(pl.multiple_of(row * BLK, BLK), BLK)
    for h in range(2):
        for yh in range(2):
            sent = []
            for c in range(2):
                at = h * 1024 + yh * 512 + c * 256
                at = slice(at, at + 256)
                acc = own_ref[:, at].astype(F32) + grad_ref[rows, at]
                acc = fb_ref[:, at].astype(F32) + acc
                chosen = jnp.broadcast_to(mask_ref[0, :, at], acc.shape) > 0.5
                sent.append(jnp.where(chosen, acc, 0.0))
            place = slice(yh * 256, yh * 256 + 256)
            mine_ref[h, :, place] = jnp.where(first, sent[0], sent[1])
            other_ref[h, :, place] = jnp.where(first, sent[1], sent[0]).astype(BF16)


def finish_kernel(
    list_ref, c_ref, mask_ref, fb_ref, own_ref, got, nxt, near_ref, far_ref,
    new_ref, step_ref, grad_ref,
):
    row = pl.program_id(0)

    @pl.when(row == 0)
    def _():
        terms = [lambda at: got[0, :, at], lambda at: nxt[:, at]]
        unpack(list_ref, 0, HALF, terms, grad_ref)

    rows = pl.ds(pl.multiple_of(row * BLK, BLK), BLK)
    for at in range(0, fb_ref.shape[1], 256):
        at = slice(at, at + 256)
        acc = own_ref[:, at].astype(F32) + grad_ref[rows, at]
        acc = fb_ref[:, at].astype(F32) + acc
        chosen = jnp.broadcast_to(mask_ref[0, :, at], acc.shape) > 0.5
        new_ref[:, at] = jnp.where(chosen, 0.0, acc).astype(BF16)
    first = c_ref[0] == 0
    for h in range(2):
        for yh in range(2):
            place = slice(yh * 256, yh * 256 + 256)
            near, far = near_ref[h, :, place], far_ref[h, :, place]
            at = h * 1024 + yh * 512
            step_ref[:, at : at + 256] = jnp.where(first, near, far)
            step_ref[:, at + 256 : at + 512] = jnp.where(first, far, near)


def state_call(body, scalars, mask, feedback, own, received, outs, out_shape, slabs=()):
    rows, cols = feedback.shape
    wide = pl.BlockSpec((BLK, cols), lambda i: (i, 0))
    line = pl.BlockSpec((1, 1, cols), lambda i: (i, 0, 0))
    slab = pl.BlockSpec((2, BLK, 512), lambda i: (i, 0, 0))
    given = [pl.BlockSpec(r.shape, lambda i, n=r.ndim: (0,) * n) for r in received]
    return pl.pallas_call(
        body,
        grid=(rows // BLK,),
        in_specs=[SMEM] * len(scalars) + [line, wide, wide] + given + [slab] * len(slabs),
        out_specs=outs,
        out_shape=out_shape,
        scratch_shapes=[pltpu.VMEM((rows, cols), F32)],
        compiler_params=pltpu.CompilerParams(vmem_limit_bytes=VMEM_LIMIT),
        cost_estimate=pl.CostEstimate(flops=1 << 22, bytes_accessed=1 << 22, transcendentals=0),
    )(*scalars, mask, feedback, own, *received, *slabs)


def chosen_sums(lists, c, mask, feedback, own, *received):
    slab = pl.BlockSpec((2, BLK, 512), lambda i: (i, 0, 0))
    shape = (8, BLK, 512)
    return state_call(
        chosen_kernel, (lists, c), mask, feedback, own, received, [slab, slab],
        [jax.ShapeDtypeStruct(shape, F32), jax.ShapeDtypeStruct(shape, BF16)],
    )


def finish(lists, c, mask, feedback, own, got, nxt, near, far):
    rows, cols = feedback.shape
    wide = pl.BlockSpec((BLK, cols), lambda i: (i, 0))
    out = jax.ShapeDtypeStruct((rows, cols), BF16)
    return state_call(
        finish_kernel, (lists, c), mask, feedback, own, (got, nxt), [wide] * 2, [out] * 2,
        (near, far),
    )


def owner_kernel(yh_ref, mine_ref, peer_ref, moment_ref, new_ref, step_ref):
    mean = (mine_ref[...].astype(F32) + peer_ref[...].astype(F32)) * (1.0 / NODES)
    moment = DECAY * moment_ref[...] + mean
    step = (mean + DECAY * moment).astype(BF16)
    for z in range(8):
        step_ref[z] = step
    own = jnp.where(yh_ref[0] == 0, moment[:, :256], moment[:, 256:])
    for b in range(4):
        new_ref[b] = own[:, b * BLK : (b + 1) * BLK]


def owner_update(yh, mine, peer, moment):
    whole = pl.BlockSpec(memory_space=pltpu.VMEM)
    return kernel_call(
        owner_kernel,
        (),
        [SMEM, whole, whole, whole],
        [whole, whole],
        [
            jax.ShapeDtypeStruct((4, BLK, BLK), F32),
            jax.ShapeDtypeStruct((8, BLK, 512), BF16),
        ],
        8 * BLK * 512,
    )(yh, mine, peer, moment)


def others_of(lists, count):
    blocks = jnp.arange(count, dtype=jnp.int32)
    left = jnp.all(lists[:, :, None] != blocks, axis=1)
    before = blocks[:, None] < blocks[None, :]
    rank = jnp.sum(jnp.where(left[:, :, None] & before, 1, 0), axis=1)
    slots = jnp.arange(count // 2, dtype=jnp.int32)
    hit = left[:, None, :] & (rank[:, None, :] == slots[None, :, None])
    return jnp.sum(jnp.where(hit, blocks, 0), axis=2)


def gather_hidden(hidden):
    far = swap(hidden, "t", 2, 4)
    near = swap(hidden, "t", 1, 4)
    return hidden, near, far, swap(far, "t", 1, 4)


def plus(kept, got):
    return (kept.astype(F32) + got.astype(F32)).astype(BF16)


def as_matrix(blocks):
    return blocks.transpose(1, 0, 2).reshape(BLK, -1)


def local(hidden, cotangent, feedback, chosen, momentum):
    rows, cols = feedback.shape[1:]
    rows_blk, cols_blk = rows // BLK, cols // BLK
    c, yh = lax.axis_index("c"), lax.axis_index("yh")
    at_c, at_yh = c.astype(jnp.int32).reshape(1), yh.astype(jnp.int32).reshape(1)
    block_of = (
        jnp.arange(rows_blk, dtype=jnp.int32)[:, None] * cols_blk
        + jnp.arange(cols, dtype=jnp.int32)[None, :] // BLK
    )
    mask = jnp.any(chosen.reshape(-1, 1, 1) == block_of[None], axis=0).astype(F32)
    moment = as_matrix(momentum[0, 0])
    mask = mask[:, None]
    picks = chosen.reshape(1, -1)
    near_picks = swap(picks, "dp", 1, 4)
    far_picks = swap(jnp.concatenate([picks, near_picks]), "dp", 3, 4)
    *shards, near_picks, far_picks = lax.optimization_barrier(
        (*gather_hidden(hidden), near_picks, far_picks)
    )
    at = (lax.axis_index("dp") ^ lax.axis_index("t")).astype(jnp.int32).reshape(1)

    def part(k, shards):
        return lax.dot_general(
            lax.select_n(at[0] ^ k, *shards),
            cotangent,
            (((0,), (0,)), ((), ())),
            preferred_element_type=F32,
        ).astype(BF16)

    (give_2,) = chosen_parts((1,), (far_picks,), (part(2, shards),))
    got_2 = swap(give_2, "dp", 2, 4)
    *shards, _ = lax.optimization_barrier((*shards, give_2))
    give_1, give_3 = chosen_parts(
        (0, 0), (near_picks, far_picks), (part(1, shards), part(3, shards))
    )
    got_1 = swap(give_1, "dp", 1, 4)
    *shards, give_3, moment = lax.optimization_barrier((*shards, give_3, moment))
    got_3 = swap(give_3, "dp", 3, 4)
    far_moment = swap(moment, "yh", 1, 2)
    others = jnp.concatenate([picks, near_picks, far_picks[1:], far_picks[:1]])
    others = others_of(others, rows_blk * cols_blk)
    rest = rest_parts(others, at, shards, cotangent)
    got_1, got_2, got_3, far_moment, give, keep, own = lax.optimization_barrier(
        (got_1, got_2, got_3, far_moment, *rest)
    )
    mine, other = chosen_sums(picks, at_c, mask, feedback[0], own, got_1, got_2, got_3)
    pair = (mine + swap(other, "c", 1, 2).astype(F32)).astype(BF16)
    pair, give = lax.optimization_barrier((pair, give))
    got_rest = swap(give, "dp", 1, 4)
    across = lax.all_to_all(pair, "z", 0, 0, tiled=True)
    near = jnp.sum(across.astype(F32), axis=0).astype(BF16)
    far = swap(near, "yh", 1, 2)
    far, give_rest = lax.optimization_barrier((far, plus(keep, got_rest[1])))
    moment = jnp.where(
        yh == 0, jnp.concatenate([moment, far_moment], 1), jnp.concatenate([far_moment, moment], 1)
    )
    momentum_new, copies = owner_update(at_yh, near, far, moment)
    next_rest = swap(give_rest, "dp", 3, 4)
    every = lax.all_to_all(copies, "z", 0, 0, tiled=True)
    feedback_new, step = finish(
        others, at_c, mask, feedback[0], own, got_rest, next_rest, every, swap(every, "c", 1, 2)
    )
    return feedback_new[None], momentum_new[None, None], step


def solution(mesh):
    fine = Mesh(mesh.devices.reshape(SHAPE), (*NODE, "dp", "t"))
    tokens = P((*NODE, "dp"), "t")
    return jax.shard_map(
        local,
        mesh=fine,
        in_specs=(
            tokens,
            tokens,
            P(NODE, "dp", "t"),
            P(NODE, "dp", "t", None),
            P("dp", "t", NODE, None, None),
        ),
        out_specs=(P(NODE, "dp", "t"), P("dp", "t", NODE, None, None), P("dp", "t")),
        check_vma=False,
    )
```

```python
import functools

import jax
import jax.numpy as jnp
from jax import lax
from jax.experimental import pallas as pl
from jax.experimental.pallas import tpu as pltpu
from jax.sharding import Mesh, PartitionSpec as P

BLK = 64
LANES = 128
HALF = 64
DECAY = 0.9
NODES = 32
F32, BF16 = jnp.float32, jnp.bfloat16
NODE = ("z", "yh", "c")
SHAPE = (8, 2, 2, 4, 4)
VMEM_LIMIT = 16 * 1024 * 1024


def swap(value, axis, flip, size):
    return lax.ppermute(value, axis, [(i, i ^ flip) for i in range(size)])


def kernel_call(body, grid, ins, outs, out_shape, cost):
    return pl.pallas_call(
        body,
        grid=grid,
        in_specs=ins,
        out_specs=outs,
        out_shape=out_shape,
        compiler_params=pltpu.CompilerParams(vmem_limit_bytes=VMEM_LIMIT),
        cost_estimate=pl.CostEstimate(flops=cost, bytes_accessed=cost, transcendentals=0),
    )


SMEM = pl.BlockSpec(memory_space=pltpu.SMEM)


def place_of(block):
    row, col = block // 32, block % 32
    rows = pl.ds(pl.multiple_of(row * BLK, BLK), BLK)
    return rows, pl.ds(pl.multiple_of(col // 2 * LANES, LANES), LANES), col % 2


def lane_halves():
    return lax.broadcasted_iota(jnp.int32, (BLK, LANES), 1) // BLK


def product(at_ref, k, shards, cot_ref, left_ref, part_ref):
    for m, shard in enumerate(shards):

        @pl.when(at_ref[0] ^ k == m)
        def _(shard=shard):
            left_ref[...] = shard[...]

    for at in range(0, cot_ref.shape[1], 512):
        part_ref[:, at : at + 512] = lax.dot_general(
            left_ref[...],
            cot_ref[:, at : at + 512],
            (((0,), (0,)), ((), ())),
            preferred_element_type=F32,
        ).astype(BF16)


def pack(list_ref, k, base, count, part_ref, out_ref, lead=None):
    upper = lane_halves() == 1

    def tile(q, carry):
        sides = []
        for side in range(2):
            rows, cols, half = place_of(list_ref[k, base + 2 * q + side])
            block = part_ref[rows, cols]
            sides.append(jnp.where(half == side, block, pltpu.roll(block, BLK, 1)))
        at = pl.ds(pl.multiple_of(q * LANES, LANES), LANES)
        value = jnp.where(upper, sides[1], sides[0])
        if lead is None:
            out_ref[:, at] = value
        else:
            out_ref[lead, :, at] = value
        return carry

    lax.fori_loop(0, count // 2, tile, 0, unroll=True)


def first_kernel(rows, *refs):
    n = len(rows)
    for row, list_ref, part_ref, out_ref in zip(rows, refs[:n], refs[n : 2 * n], refs[2 * n :]):
        pack(list_ref, row, 0, HALF, part_ref, out_ref)


def rest_kernel(
    list_ref, at_ref, s0, s1, s2, s3, cot_ref, give_1, give_2, keep_ref, own_ref, left_ref, part_ref
):
    for k, out_ref in ((1, give_1), (2, give_2), (3, keep_ref)):
        product(at_ref, k, (s0, s1, s2, s3), cot_ref, left_ref, part_ref)
        pack(list_ref, k, 0, HALF, part_ref, out_ref)
    product(at_ref, 0, (s0, s1, s2, s3), cot_ref, left_ref, own_ref)


def products_call(body, lists, at, shards, cotangent, out_shape):
    whole = pl.BlockSpec(memory_space=pltpu.VMEM)
    depth, width = shards[0].shape
    cols = cotangent.shape[1]
    return pl.pallas_call(
        body,
        in_specs=[SMEM, SMEM] + [whole] * 5,
        out_specs=jax.tree.map(lambda _: whole, out_shape),
        out_shape=out_shape,
        scratch_shapes=[pltpu.VMEM((depth, width), BF16), pltpu.VMEM((width, cols), BF16)],
        compiler_params=pltpu.CompilerParams(vmem_limit_bytes=VMEM_LIMIT),
        cost_estimate=pl.CostEstimate(flops=1 << 20, bytes_accessed=1 << 20, transcendentals=0),
    )(lists, at, *shards, cotangent)


def packed(*lead, blocks=HALF):
    return jax.ShapeDtypeStruct((*lead, BLK, blocks * BLK), BF16)


def chosen_parts(rows, lists, parts):
    whole, n = pl.BlockSpec(memory_space=pltpu.VMEM), len(rows)
    return kernel_call(
        functools.partial(first_kernel, rows),
        (),
        [SMEM] * n + [whole] * n,
        [whole] * n,
        [packed()] * n,
        1 << 20,
    )(*lists, *parts)


def rest_parts(lists, at, shards, cotangent):
    own = jax.ShapeDtypeStruct((shards[0].shape[1], cotangent.shape[1]), BF16)
    shapes = [packed(), packed(), packed(), own]
    return products_call(rest_kernel, lists, at, shards, cotangent, shapes)


def unpack(list_ref, base, count, terms, grad_ref):
    halves = lane_halves()

    def tile(q, carry):
        at = pl.ds(pl.multiple_of(q * LANES, LANES), LANES)
        value = terms[0](at).astype(F32)
        for term in terms[1:]:
            value = value + term(at).astype(F32)
        turned = pltpu.roll(value, BLK, 1)
        for side in range(2):
            rows, cols, half = place_of(list_ref[0, base + 2 * q + side])
            moved = jnp.where(half == side, value, turned)
            grad_ref[rows, cols] = jnp.where(halves == half, moved, grad_ref[rows, cols])
        return carry

    lax.fori_loop(0, count // 2, tile, 0, unroll=True)


def chosen_kernel(
    list_ref, c_ref, mask_ref, fb_ref, own_ref, got_1, got_2, got_3, mine_ref, other_ref, grad_ref
):
    row = pl.program_id(0)

    @pl.when(row == 0)
    def _():
        terms = [lambda at, ref=ref: ref[:, at] for ref in (got_1, got_2, got_3)]
        unpack(list_ref, 0, HALF, terms, grad_ref)

    first = c_ref[0] == 0
    rows = pl.ds(pl.multiple_of(row * BLK, BLK), BLK)
    for h in range(2):
        for yh in range(2):
            sent = []
            for c in range(2):
                at = h * 1024 + yh * 512 + c * 256
                at = slice(at, at + 256)
                acc = own_ref[:, at].astype(F32) + grad_ref[rows, at]
                acc = fb_ref[:, at].astype(F32) + acc
                chosen = jnp.broadcast_to(mask_ref[0, :, at], acc.shape) > 0.5
                sent.append(jnp.where(chosen, acc, 0.0))
            place = slice(yh * 256, yh * 256 + 256)
            mine_ref[h, :, place] = jnp.where(first, sent[0], sent[1])
            other_ref[h, :, place] = jnp.where(first, sent[1], sent[0]).astype(BF16)


def finish_kernel(
    list_ref, c_ref, mask_ref, fb_ref, own_ref, got, nxt, near_ref, far_ref,
    new_ref, step_ref, grad_ref,
):
    row = pl.program_id(0)

    @pl.when(row == 0)
    def _():
        terms = [lambda at: got[:, at], lambda at: nxt[:, at]]
        unpack(list_ref, 0, HALF, terms, grad_ref)

    rows = pl.ds(pl.multiple_of(row * BLK, BLK), BLK)
    for at in range(0, fb_ref.shape[1], 256):
        at = slice(at, at + 256)
        acc = own_ref[:, at].astype(F32) + grad_ref[rows, at]
        acc = fb_ref[:, at].astype(F32) + acc
        chosen = jnp.broadcast_to(mask_ref[0, :, at], acc.shape) > 0.5
        new_ref[:, at] = jnp.where(chosen, 0.0, acc).astype(BF16)
    first = c_ref[0] == 0
    for h in range(2):
        for yh in range(2):
            place = slice(yh * 256, yh * 256 + 256)
            near, far = near_ref[h, :, place], far_ref[h, :, place]
            at = h * 1024 + yh * 512
            step_ref[:, at : at + 256] = jnp.where(first, near, far)
            step_ref[:, at + 256 : at + 512] = jnp.where(first, far, near)


def state_call(body, scalars, mask, feedback, own, received, outs, out_shape, slabs=()):
    rows, cols = feedback.shape
    wide = pl.BlockSpec((BLK, cols), lambda i: (i, 0))
    line = pl.BlockSpec((1, 1, cols), lambda i: (i, 0, 0))
    slab = pl.BlockSpec((2, BLK, 512), lambda i: (i, 0, 0))
    given = [pl.BlockSpec(r.shape, lambda i, n=r.ndim: (0,) * n) for r in received]
    return pl.pallas_call(
        body,
        grid=(rows // BLK,),
        in_specs=[SMEM] * len(scalars) + [line, wide, wide] + given + [slab] * len(slabs),
        out_specs=outs,
        out_shape=out_shape,
        scratch_shapes=[pltpu.VMEM((rows, cols), F32)],
        compiler_params=pltpu.CompilerParams(vmem_limit_bytes=VMEM_LIMIT),
        cost_estimate=pl.CostEstimate(flops=1 << 22, bytes_accessed=1 << 22, transcendentals=0),
    )(*scalars, mask, feedback, own, *received, *slabs)


def chosen_sums(lists, c, mask, feedback, own, *received):
    slab = pl.BlockSpec((2, BLK, 512), lambda i: (i, 0, 0))
    shape = (8, BLK, 512)
    return state_call(
        chosen_kernel, (lists, c), mask, feedback, own, received, [slab, slab],
        [jax.ShapeDtypeStruct(shape, F32), jax.ShapeDtypeStruct(shape, BF16)],
    )


def finish(lists, c, mask, feedback, own, got, nxt, near, far):
    rows, cols = feedback.shape
    wide = pl.BlockSpec((BLK, cols), lambda i: (i, 0))
    out = jax.ShapeDtypeStruct((rows, cols), BF16)
    return state_call(
        finish_kernel, (lists, c), mask, feedback, own, (got, nxt), [wide] * 2, [out] * 2,
        (near, far),
    )


def owner_kernel(yh_ref, mine_ref, peer_ref, moment_ref, new_ref, step_ref):
    mean = (mine_ref[...].astype(F32) + peer_ref[...].astype(F32)) * (1.0 / NODES)
    moment = DECAY * moment_ref[...] + mean
    step = (mean + DECAY * moment).astype(BF16)
    for z in range(8):
        step_ref[z] = step
    own = jnp.where(yh_ref[0] == 0, moment[:, :256], moment[:, 256:])
    for b in range(4):
        new_ref[b] = own[:, b * BLK : (b + 1) * BLK]


def owner_update(yh, mine, peer, moment):
    whole = pl.BlockSpec(memory_space=pltpu.VMEM)
    return kernel_call(
        owner_kernel,
        (),
        [SMEM, whole, whole, whole],
        [whole, whole],
        [
            jax.ShapeDtypeStruct((4, BLK, BLK), F32),
            jax.ShapeDtypeStruct((8, BLK, 512), BF16),
        ],
        8 * BLK * 512,
    )(yh, mine, peer, moment)


def others_of(lists, count):
    blocks = jnp.arange(count, dtype=jnp.int32)
    left = jnp.all(lists[:, :, None] != blocks, axis=1)
    before = blocks[:, None] < blocks[None, :]
    rank = jnp.sum(jnp.where(left[:, :, None] & before, 1, 0), axis=1)
    slots = jnp.arange(count // 2, dtype=jnp.int32)
    hit = left[:, None, :] & (rank[:, None, :] == slots[None, :, None])
    return jnp.sum(jnp.where(hit, blocks, 0), axis=2)


def gather_hidden(hidden):
    far = swap(hidden, "t", 2, 4)
    near = swap(hidden, "t", 1, 4)
    return hidden, near, far, swap(far, "t", 1, 4)


def plus(kept, got):
    return (kept.astype(F32) + got.astype(F32)).astype(BF16)


def as_matrix(blocks):
    return blocks.transpose(1, 0, 2).reshape(BLK, -1)


def local(hidden, cotangent, feedback, chosen, momentum):
    rows, cols = feedback.shape[1:]
    rows_blk, cols_blk = rows // BLK, cols // BLK
    c, yh = lax.axis_index("c"), lax.axis_index("yh")
    at_c, at_yh = c.astype(jnp.int32).reshape(1), yh.astype(jnp.int32).reshape(1)
    block_of = (
        jnp.arange(rows_blk, dtype=jnp.int32)[:, None] * cols_blk
        + jnp.arange(cols, dtype=jnp.int32)[None, :] // BLK
    )
    mask = jnp.any(chosen.reshape(-1, 1, 1) == block_of[None], axis=0).astype(F32)
    moment = as_matrix(momentum[0, 0])
    mask = mask[:, None]
    picks = chosen.reshape(1, -1)
    near_picks = swap(picks, "dp", 1, 4)
    far_picks = swap(jnp.concatenate([picks, near_picks]), "dp", 3, 4)
    *shards, near_picks, far_picks = lax.optimization_barrier(
        (*gather_hidden(hidden), near_picks, far_picks)
    )
    at = (lax.axis_index("dp") ^ lax.axis_index("t")).astype(jnp.int32).reshape(1)

    def part(k, shards):
        return lax.dot_general(
            lax.select_n(at[0] ^ k, *shards),
            cotangent,
            (((0,), (0,)), ((), ())),
            preferred_element_type=F32,
        ).astype(BF16)

    (give_2,) = chosen_parts((1,), (far_picks,), (part(2, shards),))
    got_2 = swap(give_2, "dp", 2, 4)
    *shards, _ = lax.optimization_barrier((*shards, give_2))
    give_1, give_3 = chosen_parts(
        (0, 0), (near_picks, far_picks), (part(1, shards), part(3, shards))
    )
    got_1 = swap(give_1, "dp", 1, 4)
    *shards, give_3, moment = lax.optimization_barrier((*shards, give_3, moment))
    got_3 = swap(give_3, "dp", 3, 4)
    far_moment = swap(moment, "yh", 1, 2)
    others = jnp.concatenate([picks, near_picks, far_picks[1:], far_picks[:1]])
    others = others_of(others, rows_blk * cols_blk)
    rest = rest_parts(others, at, shards, cotangent)
    got_1, got_2, got_3, far_moment, give_1, give_2, keep, own = lax.optimization_barrier(
        (got_1, got_2, got_3, far_moment, *rest)
    )
    mine, other = chosen_sums(picks, at_c, mask, feedback[0], own, got_1, got_2, got_3)
    pair = (mine + swap(other, "c", 1, 2).astype(F32)).astype(BF16)
    pair, give_1, give_2 = lax.optimization_barrier((pair, give_1, give_2))
    via = swap(give_2, "dp", 1, 4)
    across = lax.all_to_all(pair, "z", 0, 0, tiled=True)
    near = jnp.sum(across.astype(F32), axis=0).astype(BF16)
    far = swap(near, "yh", 1, 2)
    far, give_3 = lax.optimization_barrier((far, plus(keep, via)))
    moment = jnp.where(
        yh == 0, jnp.concatenate([moment, far_moment], 1), jnp.concatenate([far_moment, moment], 1)
    )
    momentum_new, copies = owner_update(at_yh, near, far, moment)
    got_rest, next_rest = swap(give_1, "dp", 1, 4), swap(give_3, "dp", 3, 4)
    every = lax.all_to_all(copies, "z", 0, 0, tiled=True)
    feedback_new, step = finish(
        others, at_c, mask, feedback[0], own, got_rest, next_rest, every, swap(every, "c", 1, 2)
    )
    return feedback_new[None], momentum_new[None, None], step


def solution(mesh):
    fine = Mesh(mesh.devices.reshape(SHAPE), (*NODE, "dp", "t"))
    tokens = P((*NODE, "dp"), "t")
    return jax.shard_map(
        local,
        mesh=fine,
        in_specs=(
            tokens,
            tokens,
            P(NODE, "dp", "t"),
            P(NODE, "dp", "t", None),
            P("dp", "t", NODE, None, None),
        ),
        out_specs=(P(NODE, "dp", "t"), P("dp", "t", NODE, None, None), P("dp", "t")),
        check_vma=False,
    )
```

```python
import functools

import jax
import jax.numpy as jnp
from jax import lax
from jax.experimental import pallas as pl
from jax.experimental.pallas import tpu as pltpu
from jax.sharding import Mesh, PartitionSpec as P

BLK = 64
LANES = 128
HALF = 64
DECAY = 0.9
NODES = 32
F32, BF16 = jnp.float32, jnp.bfloat16
NODE = ("z", "yh", "c")
SHAPE = (8, 2, 2, 4, 4)
VMEM_LIMIT = 16 * 1024 * 1024


def swap(value, axis, flip, size):
    return lax.ppermute(value, axis, [(i, i ^ flip) for i in range(size)])


def kernel_call(body, grid, ins, outs, out_shape, cost):
    return pl.pallas_call(
        body,
        grid=grid,
        in_specs=ins,
        out_specs=outs,
        out_shape=out_shape,
        compiler_params=pltpu.CompilerParams(vmem_limit_bytes=VMEM_LIMIT),
        cost_estimate=pl.CostEstimate(flops=cost, bytes_accessed=cost, transcendentals=0),
    )


SMEM = pl.BlockSpec(memory_space=pltpu.SMEM)


def place_of(block):
    row, col = block // 32, block % 32
    rows = pl.ds(pl.multiple_of(row * BLK, BLK), BLK)
    return rows, pl.ds(pl.multiple_of(col // 2 * LANES, LANES), LANES), col % 2


def lane_halves():
    return lax.broadcasted_iota(jnp.int32, (BLK, LANES), 1) // BLK


def product(at_ref, k, shards, cot_ref, left_ref, part_ref):
    for m, shard in enumerate(shards):

        @pl.when(at_ref[0] ^ k == m)
        def _(shard=shard):
            left_ref[...] = shard[...]

    for at in range(0, cot_ref.shape[1], 512):
        part_ref[:, at : at + 512] = lax.dot_general(
            left_ref[...],
            cot_ref[:, at : at + 512],
            (((0,), (0,)), ((), ())),
            preferred_element_type=F32,
        ).astype(BF16)


def pack(list_ref, k, base, count, part_ref, out_ref, lead=None):
    upper = lane_halves() == 1

    def tile(q, carry):
        sides = []
        for side in range(2):
            rows, cols, half = place_of(list_ref[k, base + 2 * q + side])
            block = part_ref[rows, cols]
            sides.append(jnp.where(half == side, block, pltpu.roll(block, BLK, 1)))
        at = pl.ds(pl.multiple_of(q * LANES, LANES), LANES)
        value = jnp.where(upper, sides[1], sides[0])
        if lead is None:
            out_ref[:, at] = value
        else:
            out_ref[lead, :, at] = value
        return carry

    lax.fori_loop(0, count // 2, tile, 0, unroll=True)


def first_kernel(rows, *refs):
    n = len(rows)
    for row, list_ref, part_ref, out_ref in zip(rows, refs[:n], refs[n : 2 * n], refs[2 * n :]):
        pack(list_ref, row, 0, HALF, part_ref, out_ref)


def rest_kernel(
    list_ref, at_ref, s0, s1, s2, s3, cot_ref, give_1, give_2, keep_ref, own_ref, left_ref, part_ref
):
    for k, out_ref in ((1, give_1), (2, give_2), (3, keep_ref)):
        product(at_ref, k, (s0, s1, s2, s3), cot_ref, left_ref, part_ref)
        pack(list_ref, k, 0, HALF, part_ref, out_ref)
    product(at_ref, 0, (s0, s1, s2, s3), cot_ref, left_ref, own_ref)


def products_call(body, lists, at, shards, cotangent, out_shape):
    whole = pl.BlockSpec(memory_space=pltpu.VMEM)
    depth, width = shards[0].shape
    cols = cotangent.shape[1]
    return pl.pallas_call(
        body,
        in_specs=[SMEM, SMEM] + [whole] * 5,
        out_specs=jax.tree.map(lambda _: whole, out_shape),
        out_shape=out_shape,
        scratch_shapes=[pltpu.VMEM((depth, width), BF16), pltpu.VMEM((width, cols), BF16)],
        compiler_params=pltpu.CompilerParams(vmem_limit_bytes=VMEM_LIMIT),
        cost_estimate=pl.CostEstimate(flops=1 << 20, bytes_accessed=1 << 20, transcendentals=0),
    )(lists, at, *shards, cotangent)


def packed(*lead, blocks=HALF):
    return jax.ShapeDtypeStruct((*lead, BLK, blocks * BLK), BF16)


def chosen_parts(rows, lists, parts):
    whole, n = pl.BlockSpec(memory_space=pltpu.VMEM), len(rows)
    return kernel_call(
        functools.partial(first_kernel, rows),
        (),
        [SMEM] * n + [whole] * n,
        [whole] * n,
        [packed()] * n,
        1 << 20,
    )(*lists, *parts)


def rest_parts(lists, at, shards, cotangent):
    own = jax.ShapeDtypeStruct((shards[0].shape[1], cotangent.shape[1]), BF16)
    shapes = [packed(), packed(), packed(), own]
    return products_call(rest_kernel, lists, at, shards, cotangent, shapes)


def unpack(list_ref, base, count, terms, grad_ref):
    halves = lane_halves()

    def tile(q, carry):
        at = pl.ds(pl.multiple_of(q * LANES, LANES), LANES)
        value = terms[0](at).astype(F32)
        for term in terms[1:]:
            value = value + term(at).astype(F32)
        turned = pltpu.roll(value, BLK, 1)
        for side in range(2):
            rows, cols, half = place_of(list_ref[0, base + 2 * q + side])
            moved = jnp.where(half == side, value, turned)
            grad_ref[rows, cols] = jnp.where(halves == half, moved, grad_ref[rows, cols])
        return carry

    lax.fori_loop(0, count // 2, tile, 0, unroll=True)


def chosen_kernel(
    list_ref, c_ref, mask_ref, fb_ref, own_ref, got_1, got_2, got_3, mine_ref, other_ref, grad_ref
):
    row = pl.program_id(0)

    @pl.when(row == 0)
    def _():
        terms = [lambda at, ref=ref: ref[:, at] for ref in (got_1, got_2, got_3)]
        unpack(list_ref, 0, HALF, terms, grad_ref)

    first = c_ref[0] == 0
    rows = pl.ds(pl.multiple_of(row * BLK, BLK), BLK)
    for h in range(2):
        for yh in range(2):
            sent = []
            for c in range(2):
                at = h * 1024 + yh * 512 + c * 256
                at = slice(at, at + 256)
                acc = own_ref[:, at].astype(F32) + grad_ref[rows, at]
                acc = fb_ref[:, at].astype(F32) + acc
                chosen = jnp.broadcast_to(mask_ref[0, :, at], acc.shape) > 0.5
                sent.append(jnp.where(chosen, acc, 0.0))
            place = slice(yh * 256, yh * 256 + 256)
            mine_ref[h, :, place] = jnp.where(first, sent[0], sent[1])
            other_ref[h, :, place] = jnp.where(first, sent[1], sent[0]).astype(BF16)


def finish_kernel(
    list_ref, c_ref, mask_ref, fb_ref, own_ref, got, nxt, near_ref, far_ref,
    new_ref, step_ref, grad_ref,
):
    row = pl.program_id(0)

    @pl.when(row == 0)
    def _():
        terms = [lambda at: got[:, at], lambda at: nxt[:, at]]
        unpack(list_ref, 0, HALF, terms, grad_ref)

    rows = pl.ds(pl.multiple_of(row * BLK, BLK), BLK)
    for at in range(0, fb_ref.shape[1], 256):
        at = slice(at, at + 256)
        acc = own_ref[:, at].astype(F32) + grad_ref[rows, at]
        acc = fb_ref[:, at].astype(F32) + acc
        chosen = jnp.broadcast_to(mask_ref[0, :, at], acc.shape) > 0.5
        new_ref[:, at] = jnp.where(chosen, 0.0, acc).astype(BF16)
    first = c_ref[0] == 0
    for h in range(2):
        for yh in range(2):
            place = slice(yh * 256, yh * 256 + 256)
            near, far = near_ref[h, :, place], far_ref[h, :, place]
            at = h * 1024 + yh * 512
            step_ref[:, at : at + 256] = jnp.where(first, near, far)
            step_ref[:, at + 256 : at + 512] = jnp.where(first, far, near)


def state_call(body, scalars, mask, feedback, own, received, outs, out_shape, slabs=()):
    rows, cols = feedback.shape
    wide = pl.BlockSpec((BLK, cols), lambda i: (i, 0))
    line = pl.BlockSpec((1, 1, cols), lambda i: (i, 0, 0))
    slab = pl.BlockSpec((2, BLK, 512), lambda i: (i, 0, 0))
    given = [pl.BlockSpec(r.shape, lambda i, n=r.ndim: (0,) * n) for r in received]
    return pl.pallas_call(
        body,
        grid=(rows // BLK,),
        in_specs=[SMEM] * len(scalars) + [line, wide, wide] + given + [slab] * len(slabs),
        out_specs=outs,
        out_shape=out_shape,
        scratch_shapes=[pltpu.VMEM((rows, cols), F32)],
        compiler_params=pltpu.CompilerParams(vmem_limit_bytes=VMEM_LIMIT),
        cost_estimate=pl.CostEstimate(flops=1 << 22, bytes_accessed=1 << 22, transcendentals=0),
    )(*scalars, mask, feedback, own, *received, *slabs)


def chosen_sums(lists, c, mask, feedback, own, *received):
    slab = pl.BlockSpec((2, BLK, 512), lambda i: (i, 0, 0))
    shape = (8, BLK, 512)
    return state_call(
        chosen_kernel, (lists, c), mask, feedback, own, received, [slab, slab],
        [jax.ShapeDtypeStruct(shape, F32), jax.ShapeDtypeStruct(shape, BF16)],
    )


def finish(lists, c, mask, feedback, own, got, nxt, near, far):
    rows, cols = feedback.shape
    wide = pl.BlockSpec((BLK, cols), lambda i: (i, 0))
    out = jax.ShapeDtypeStruct((rows, cols), BF16)
    return state_call(
        finish_kernel, (lists, c), mask, feedback, own, (got, nxt), [wide] * 2, [out] * 2,
        (near, far),
    )


def owner_kernel(yh_ref, mine_ref, peer_ref, moment_ref, new_ref, step_ref):
    mean = (mine_ref[...].astype(F32) + peer_ref[...].astype(F32)) * (1.0 / NODES)
    moment = DECAY * moment_ref[...] + mean
    step = (mean + DECAY * moment).astype(BF16)
    for z in range(8):
        step_ref[z] = step
    own = jnp.where(yh_ref[0] == 0, moment[:, :256], moment[:, 256:])
    for b in range(4):
        new_ref[b] = own[:, b * BLK : (b + 1) * BLK]


def owner_update(yh, mine, peer, moment):
    whole = pl.BlockSpec(memory_space=pltpu.VMEM)
    return kernel_call(
        owner_kernel,
        (),
        [SMEM, whole, whole, whole],
        [whole, whole],
        [
            jax.ShapeDtypeStruct((4, BLK, BLK), F32),
            jax.ShapeDtypeStruct((8, BLK, 512), BF16),
        ],
        8 * BLK * 512,
    )(yh, mine, peer, moment)


def others_of(lists, count):
    blocks = jnp.arange(count, dtype=jnp.int32)
    left = jnp.all(lists[:, :, None] != blocks, axis=1)
    before = blocks[:, None] < blocks[None, :]
    rank = jnp.sum(jnp.where(left[:, :, None] & before, 1, 0), axis=1)
    slots = jnp.arange(count // 2, dtype=jnp.int32)
    hit = left[:, None, :] & (rank[:, None, :] == slots[None, :, None])
    return jnp.sum(jnp.where(hit, blocks, 0), axis=2)


def gather_hidden(hidden):
    far = swap(hidden, "t", 2, 4)
    near = swap(hidden, "t", 1, 4)
    return hidden, near, far, swap(far, "t", 1, 4)


def plus(kept, got):
    return (kept.astype(F32) + got.astype(F32)).astype(BF16)


def as_matrix(blocks):
    return blocks.transpose(1, 0, 2).reshape(BLK, -1)


def local(hidden, cotangent, feedback, chosen, momentum):
    rows, cols = feedback.shape[1:]
    rows_blk, cols_blk = rows // BLK, cols // BLK
    c, yh = lax.axis_index("c"), lax.axis_index("yh")
    at_c, at_yh = c.astype(jnp.int32).reshape(1), yh.astype(jnp.int32).reshape(1)
    block_of = (
        jnp.arange(rows_blk, dtype=jnp.int32)[:, None] * cols_blk
        + jnp.arange(cols, dtype=jnp.int32)[None, :] // BLK
    )
    mask = jnp.any(chosen.reshape(-1, 1, 1) == block_of[None], axis=0).astype(F32)
    moment = as_matrix(momentum[0, 0])
    mask = mask[:, None]
    picks = chosen.reshape(1, -1)
    far_picks = swap(picks, "dp", 2, 4)
    near_picks = swap(jnp.concatenate([picks, far_picks]), "dp", 1, 4)
    *shards, far_picks = lax.optimization_barrier((*gather_hidden(hidden), far_picks))
    at = (lax.axis_index("dp") ^ lax.axis_index("t")).astype(jnp.int32).reshape(1)

    def part(k, shards):
        return lax.dot_general(
            lax.select_n(at[0] ^ k, *shards),
            cotangent,
            (((0,), (0,)), ((), ())),
            preferred_element_type=F32,
        ).astype(BF16)

    (give_2,) = chosen_parts((0,), (far_picks,), (part(2, shards),))
    got_2 = swap(give_2, "dp", 2, 4)
    *shards, _ = lax.optimization_barrier((*shards, give_2))
    give_1, give_3 = chosen_parts(
        (0, 1), (near_picks, near_picks), (part(1, shards), part(3, shards))
    )
    got_1 = swap(give_1, "dp", 1, 4)
    *shards, give_3, moment = lax.optimization_barrier((*shards, give_3, moment))
    got_3 = swap(give_3, "dp", 3, 4)
    far_moment = swap(moment, "yh", 1, 2)
    others = jnp.concatenate([picks, near_picks[:1], far_picks, near_picks[1:]])
    others = others_of(others, rows_blk * cols_blk)
    rest = rest_parts(others, at, shards, cotangent)
    got_1, got_2, got_3, far_moment, give_1, give_2, keep, own = lax.optimization_barrier(
        (got_1, got_2, got_3, far_moment, *rest)
    )
    mine, other = chosen_sums(picks, at_c, mask, feedback[0], own, got_1, got_2, got_3)
    pair = (mine + swap(other, "c", 1, 2).astype(F32)).astype(BF16)
    pair, give_1, give_2 = lax.optimization_barrier((pair, give_1, give_2))
    via = swap(give_2, "dp", 1, 4)
    across = lax.all_to_all(pair, "z", 0, 0, tiled=True)
    near = jnp.sum(across.astype(F32), axis=0).astype(BF16)
    far = swap(near, "yh", 1, 2)
    far, give_3 = lax.optimization_barrier((far, plus(keep, via)))
    moment = jnp.where(
        yh == 0, jnp.concatenate([moment, far_moment], 1), jnp.concatenate([far_moment, moment], 1)
    )
    momentum_new, copies = owner_update(at_yh, near, far, moment)
    got_rest, next_rest = swap(give_1, "dp", 1, 4), swap(give_3, "dp", 3, 4)
    every = lax.all_to_all(copies, "z", 0, 0, tiled=True)
    feedback_new, step = finish(
        others, at_c, mask, feedback[0], own, got_rest, next_rest, every, swap(every, "c", 1, 2)
    )
    return feedback_new[None], momentum_new[None, None], step


def solution(mesh):
    fine = Mesh(mesh.devices.reshape(SHAPE), (*NODE, "dp", "t"))
    tokens = P((*NODE, "dp"), "t")
    return jax.shard_map(
        local,
        mesh=fine,
        in_specs=(
            tokens,
            tokens,
            P(NODE, "dp", "t"),
            P(NODE, "dp", "t", None),
            P("dp", "t", NODE, None, None),
        ),
        out_specs=(P(NODE, "dp", "t"), P("dp", "t", NODE, None, None), P("dp", "t")),
        check_vma=False,
    )
```

```python
import functools

import jax
import jax.numpy as jnp
from jax import lax
from jax.experimental import pallas as pl
from jax.experimental.pallas import tpu as pltpu
from jax.sharding import Mesh, PartitionSpec as P

BLK = 64
LANES = 128
HALF = 64
DECAY = 0.9
NODES = 32
F32, BF16 = jnp.float32, jnp.bfloat16
NODE = ("z", "yh", "c")
SHAPE = (8, 2, 2, 4, 4)
VMEM_LIMIT = 16 * 1024 * 1024


def swap(value, axis, flip, size):
    return lax.ppermute(value, axis, [(i, i ^ flip) for i in range(size)])


def kernel_call(body, grid, ins, outs, out_shape, cost):
    return pl.pallas_call(
        body,
        grid=grid,
        in_specs=ins,
        out_specs=outs,
        out_shape=out_shape,
        compiler_params=pltpu.CompilerParams(vmem_limit_bytes=VMEM_LIMIT),
        cost_estimate=pl.CostEstimate(flops=cost, bytes_accessed=cost, transcendentals=0),
    )


SMEM = pl.BlockSpec(memory_space=pltpu.SMEM)


def place_of(block):
    row, col = block // 32, block % 32
    rows = pl.ds(pl.multiple_of(row * BLK, BLK), BLK)
    return rows, pl.ds(pl.multiple_of(col // 2 * LANES, LANES), LANES), col % 2


def lane_halves():
    return lax.broadcasted_iota(jnp.int32, (BLK, LANES), 1) // BLK


def product(at_ref, k, shards, cot_ref, left_ref, part_ref):
    for m, shard in enumerate(shards):

        @pl.when(at_ref[0] ^ k == m)
        def _(shard=shard):
            left_ref[...] = shard[...]

    for at in range(0, cot_ref.shape[1], 512):
        part_ref[:, at : at + 512] = lax.dot_general(
            left_ref[...],
            cot_ref[:, at : at + 512],
            (((0,), (0,)), ((), ())),
            preferred_element_type=F32,
        ).astype(BF16)


def pack(list_ref, k, base, count, part_ref, out_ref, lead=None):
    upper = lane_halves() == 1

    def tile(q, carry):
        sides = []
        for side in range(2):
            rows, cols, half = place_of(list_ref[k, base + 2 * q + side])
            block = part_ref[rows, cols]
            sides.append(jnp.where(half == side, block, pltpu.roll(block, BLK, 1)))
        at = pl.ds(pl.multiple_of(q * LANES, LANES), LANES)
        value = jnp.where(upper, sides[1], sides[0])
        if lead is None:
            out_ref[:, at] = value
        else:
            out_ref[lead, :, at] = value
        return carry

    lax.fori_loop(0, count // 2, tile, 0, unroll=True)


def first_kernel(rows, *refs):
    n = len(rows)
    for row, list_ref, part_ref, out_ref in zip(rows, refs[:n], refs[n : 2 * n], refs[2 * n :]):
        pack(list_ref, row, 0, HALF, part_ref, out_ref)


def rest_kernel(
    list_ref, at_ref, s0, s1, s2, s3, cot_ref, give_1, give_2, keep_ref, own_ref, left_ref, part_ref
):
    for k, out_ref in ((1, give_1), (2, give_2), (3, keep_ref)):
        product(at_ref, k, (s0, s1, s2, s3), cot_ref, left_ref, part_ref)
        pack(list_ref, k, 0, HALF, part_ref, out_ref)
    product(at_ref, 0, (s0, s1, s2, s3), cot_ref, left_ref, own_ref)


def products_call(body, lists, at, shards, cotangent, out_shape):
    whole = pl.BlockSpec(memory_space=pltpu.VMEM)
    depth, width = shards[0].shape
    cols = cotangent.shape[1]
    return pl.pallas_call(
        body,
        in_specs=[SMEM, SMEM] + [whole] * 5,
        out_specs=jax.tree.map(lambda _: whole, out_shape),
        out_shape=out_shape,
        scratch_shapes=[pltpu.VMEM((depth, width), BF16), pltpu.VMEM((width, cols), BF16)],
        compiler_params=pltpu.CompilerParams(vmem_limit_bytes=VMEM_LIMIT),
        cost_estimate=pl.CostEstimate(flops=1 << 20, bytes_accessed=1 << 20, transcendentals=0),
    )(lists, at, *shards, cotangent)


def packed(*lead, blocks=HALF):
    return jax.ShapeDtypeStruct((*lead, BLK, blocks * BLK), BF16)


def chosen_parts(rows, lists, parts):
    whole, n = pl.BlockSpec(memory_space=pltpu.VMEM), len(rows)
    return kernel_call(
        functools.partial(first_kernel, rows),
        (),
        [SMEM] * n + [whole] * n,
        [whole] * n,
        [packed()] * n,
        1 << 20,
    )(*lists, *parts)


def rest_parts(lists, at, shards, cotangent):
    own = jax.ShapeDtypeStruct((shards[0].shape[1], cotangent.shape[1]), BF16)
    shapes = [packed(), packed(), packed(), own]
    return products_call(rest_kernel, lists, at, shards, cotangent, shapes)


def unpack(list_ref, base, count, terms, grad_ref):
    halves = lane_halves()

    def tile(q, carry):
        at = pl.ds(pl.multiple_of(q * LANES, LANES), LANES)
        value = terms[0](at).astype(F32)
        for term in terms[1:]:
            value = value + term(at).astype(F32)
        turned = pltpu.roll(value, BLK, 1)
        for side in range(2):
            rows, cols, half = place_of(list_ref[0, base + 2 * q + side])
            moved = jnp.where(half == side, value, turned)
            grad_ref[rows, cols] = jnp.where(halves == half, moved, grad_ref[rows, cols])
        return carry

    lax.fori_loop(0, count // 2, tile, 0, unroll=True)


def chosen_kernel(
    list_ref, c_ref, mask_ref, fb_ref, own_ref, got_1, got_2, got_3, mine_ref, other_ref, grad_ref
):
    row = pl.program_id(0)

    @pl.when(row == 0)
    def _():
        terms = [lambda at, ref=ref: ref[:, at] for ref in (got_1, got_2, got_3)]
        unpack(list_ref, 0, HALF, terms, grad_ref)

    first = c_ref[0] == 0
    rows = pl.ds(pl.multiple_of(row * BLK, BLK), BLK)
    for h in range(2):
        for yh in range(2):
            sent = []
            for c in range(2):
                at = h * 1024 + yh * 512 + c * 256
                at = slice(at, at + 256)
                acc = own_ref[:, at].astype(F32) + grad_ref[rows, at]
                acc = fb_ref[:, at].astype(F32) + acc
                chosen = jnp.broadcast_to(mask_ref[0, :, at], acc.shape) > 0.5
                sent.append(jnp.where(chosen, acc, 0.0))
            place = slice(yh * 256, yh * 256 + 256)
            mine_ref[h, :, place] = jnp.where(first, sent[0], sent[1])
            other_ref[h, :, place] = jnp.where(first, sent[1], sent[0]).astype(BF16)


def finish_kernel(
    list_ref, c_ref, mask_ref, fb_ref, own_ref, got, nxt, near_ref, far_ref,
    new_ref, step_ref, grad_ref,
):
    row = pl.program_id(0)

    @pl.when(row == 0)
    def _():
        terms = [lambda at: got[:, at], lambda at: nxt[:, at]]
        unpack(list_ref, 0, HALF, terms, grad_ref)

    rows = pl.ds(pl.multiple_of(row * BLK, BLK), BLK)
    for at in range(0, fb_ref.shape[1], 256):
        at = slice(at, at + 256)
        acc = own_ref[:, at].astype(F32) + grad_ref[rows, at]
        acc = fb_ref[:, at].astype(F32) + acc
        chosen = jnp.broadcast_to(mask_ref[0, :, at], acc.shape) > 0.5
        new_ref[:, at] = jnp.where(chosen, 0.0, acc).astype(BF16)
    first = c_ref[0] == 0
    for h in range(2):
        for yh in range(2):
            place = slice(yh * 256, yh * 256 + 256)
            near, far = near_ref[h, :, place], far_ref[h, :, place]
            at = h * 1024 + yh * 512
            step_ref[:, at : at + 256] = jnp.where(first, near, far)
            step_ref[:, at + 256 : at + 512] = jnp.where(first, far, near)


def state_call(body, scalars, mask, feedback, own, received, outs, out_shape, slabs=()):
    rows, cols = feedback.shape
    wide = pl.BlockSpec((BLK, cols), lambda i: (i, 0))
    line = pl.BlockSpec((1, 1, cols), lambda i: (i, 0, 0))
    slab = pl.BlockSpec((2, BLK, 512), lambda i: (i, 0, 0))
    given = [pl.BlockSpec(r.shape, lambda i, n=r.ndim: (0,) * n) for r in received]
    return pl.pallas_call(
        body,
        grid=(rows // BLK,),
        in_specs=[SMEM] * len(scalars) + [line, wide, wide] + given + [slab] * len(slabs),
        out_specs=outs,
        out_shape=out_shape,
        scratch_shapes=[pltpu.VMEM((rows, cols), F32)],
        compiler_params=pltpu.CompilerParams(vmem_limit_bytes=VMEM_LIMIT),
        cost_estimate=pl.CostEstimate(flops=1 << 22, bytes_accessed=1 << 22, transcendentals=0),
    )(*scalars, mask, feedback, own, *received, *slabs)


def chosen_sums(lists, c, mask, feedback, own, *received):
    slab = pl.BlockSpec((2, BLK, 512), lambda i: (i, 0, 0))
    shape = (8, BLK, 512)
    return state_call(
        chosen_kernel, (lists, c), mask, feedback, own, received, [slab, slab],
        [jax.ShapeDtypeStruct(shape, F32), jax.ShapeDtypeStruct(shape, BF16)],
    )


def finish(lists, c, mask, feedback, own, got, nxt, near, far):
    rows, cols = feedback.shape
    wide = pl.BlockSpec((BLK, cols), lambda i: (i, 0))
    out = jax.ShapeDtypeStruct((rows, cols), BF16)
    return state_call(
        finish_kernel, (lists, c), mask, feedback, own, (got, nxt), [wide] * 2, [out] * 2,
        (near, far),
    )


def owner_kernel(yh_ref, mine_ref, peer_ref, moment_ref, new_ref, step_ref):
    mean = (mine_ref[...].astype(F32) + peer_ref[...].astype(F32)) * (1.0 / NODES)
    moment = DECAY * moment_ref[...] + mean
    step = (mean + DECAY * moment).astype(BF16)
    for z in range(8):
        step_ref[z] = step
    own = jnp.where(yh_ref[0] == 0, moment[:, :256], moment[:, 256:])
    for b in range(4):
        new_ref[b] = own[:, b * BLK : (b + 1) * BLK]


def owner_update(yh, mine, peer, moment):
    whole = pl.BlockSpec(memory_space=pltpu.VMEM)
    return kernel_call(
        owner_kernel,
        (),
        [SMEM, whole, whole, whole],
        [whole, whole],
        [
            jax.ShapeDtypeStruct((4, BLK, BLK), F32),
            jax.ShapeDtypeStruct((8, BLK, 512), BF16),
        ],
        8 * BLK * 512,
    )(yh, mine, peer, moment)


def others_of(lists, count):
    blocks = jnp.arange(count, dtype=jnp.int32)
    left = jnp.all(lists[:, :, None] != blocks, axis=1)
    before = blocks[:, None] < blocks[None, :]
    rank = jnp.sum(jnp.where(left[:, :, None] & before, 1, 0), axis=1)
    slots = jnp.arange(count // 2, dtype=jnp.int32)
    hit = left[:, None, :] & (rank[:, None, :] == slots[None, :, None])
    return jnp.sum(jnp.where(hit, blocks, 0), axis=2)


def gather_hidden(hidden):
    far = swap(hidden, "t", 2, 4)
    near = swap(hidden, "t", 1, 4)
    return hidden, near, far, swap(far, "t", 1, 4)


def plus(kept, got):
    return (kept.astype(F32) + got.astype(F32)).astype(BF16)


def as_matrix(blocks):
    return blocks.transpose(1, 0, 2).reshape(BLK, -1)


def local(hidden, cotangent, feedback, chosen, momentum):
    rows, cols = feedback.shape[1:]
    rows_blk, cols_blk = rows // BLK, cols // BLK
    c, yh = lax.axis_index("c"), lax.axis_index("yh")
    at_c, at_yh = c.astype(jnp.int32).reshape(1), yh.astype(jnp.int32).reshape(1)
    block_of = (
        jnp.arange(rows_blk, dtype=jnp.int32)[:, None] * cols_blk
        + jnp.arange(cols, dtype=jnp.int32)[None, :] // BLK
    )
    mask = jnp.any(chosen.reshape(-1, 1, 1) == block_of[None], axis=0).astype(F32)
    moment = as_matrix(momentum[0, 0])
    mask = mask[:, None]
    picks = chosen.reshape(1, -1)
    far_picks = swap(picks, "dp", 2, 4)
    near_picks = swap(jnp.concatenate([picks, far_picks]), "dp", 1, 4)
    *shards, far_picks = lax.optimization_barrier((*gather_hidden(hidden), far_picks))
    at = (lax.axis_index("dp") ^ lax.axis_index("t")).astype(jnp.int32).reshape(1)

    def part(k, shards):
        return lax.dot_general(
            lax.select_n(at[0] ^ k, *shards),
            cotangent,
            (((0,), (0,)), ((), ())),
            preferred_element_type=F32,
        ).astype(BF16)

    (give_2,) = chosen_parts((0,), (far_picks,), (part(2, shards),))
    got_2 = swap(give_2, "dp", 2, 4)
    *shards, _ = lax.optimization_barrier((*shards, give_2))
    give_1, give_3 = chosen_parts(
        (0, 1), (near_picks, near_picks), (part(1, shards), part(3, shards))
    )
    got_1 = swap(give_1, "dp", 1, 4)
    *shards, give_3, moment = lax.optimization_barrier((*shards, give_3, moment))
    got_3 = swap(give_3, "dp", 3, 4)
    others = jnp.concatenate([picks, near_picks[:1], far_picks, near_picks[1:]])
    others = others_of(others, rows_blk * cols_blk)
    rest = rest_parts(others, at, shards, cotangent)
    got_1, got_2, got_3, give_1, give_2, keep, own = lax.optimization_barrier(
        (got_1, got_2, got_3, *rest)
    )
    mine, other = chosen_sums(picks, at_c, mask, feedback[0], own, got_1, got_2, got_3)
    pair = (mine + swap(other, "c", 1, 2).astype(F32)).astype(BF16)
    pair, give_1, give_2, moment = lax.optimization_barrier((pair, give_1, give_2, moment))
    far_moment = swap(moment, "yh", 1, 2)
    via = swap(give_2, "dp", 1, 4)
    across = lax.all_to_all(pair, "z", 0, 0, tiled=True)
    near = jnp.sum(across.astype(F32), axis=0).astype(BF16)
    far = swap(near, "yh", 1, 2)
    far, give_3 = lax.optimization_barrier((far, plus(keep, via)))
    moment = jnp.where(
        yh == 0, jnp.concatenate([moment, far_moment], 1), jnp.concatenate([far_moment, moment], 1)
    )
    momentum_new, copies = owner_update(at_yh, near, far, moment)
    got_rest, next_rest = swap(give_1, "dp", 1, 4), swap(give_3, "dp", 3, 4)
    every = lax.all_to_all(copies, "z", 0, 0, tiled=True)
    feedback_new, step = finish(
        others, at_c, mask, feedback[0], own, got_rest, next_rest, every, swap(every, "c", 1, 2)
    )
    return feedback_new[None], momentum_new[None, None], step


def solution(mesh):
    fine = Mesh(mesh.devices.reshape(SHAPE), (*NODE, "dp", "t"))
    tokens = P((*NODE, "dp"), "t")
    return jax.shard_map(
        local,
        mesh=fine,
        in_specs=(
            tokens,
            tokens,
            P(NODE, "dp", "t"),
            P(NODE, "dp", "t", None),
            P("dp", "t", NODE, None, None),
        ),
        out_specs=(P(NODE, "dp", "t"), P("dp", "t", NODE, None, None), P("dp", "t")),
        check_vma=False,
    )
```
